512 devices in a mesh: seq: 32 (over y, x), section: 16 (over z, core).
Axes of the slice: x: 4, y: 8, z: 8, core: 2. Of those that a mesh axis runs over, the one named last changes fastest.
Arguments:
- fwd_input: bfloat16 [16, 2048, 1024], P('section', 'seq'), may hold values from -6 to 6
- bwd_input: bfloat16 [16, 2048, 1024], P('section', 'seq'), may hold values from -6 to 6
- bwd_grad: float32 [16, 2048, 1024], P('section', 'seq'), may hold values from -6 to 6
- norm_gain: float32 [16, 1024], P('section'), may hold values from 0.5 to 2.5
- w_query: bfloat16 [16, 1024, 1024], P('section', 'seq'), may hold values from -1 to 1
- w_key: bfloat16 [16, 1024, 1024], P('section', 'seq'), may hold values from -1 to 1
- w_value: bfloat16 [16, 1024, 1024], P('section', 'seq'), may hold values from -0.1875 to 0.1875
- w_out: bfloat16 [16, 1024, 1024], P('section', 'seq'), may hold values from -0.1875 to 0.1875
Outputs:
- next_input: bfloat16 [16, 2048, 1024], P('section', 'seq')
- prev_grad: float32 [16, 2048, 1024], P('section', 'seq')
The draws below stay inside these ranges and needn't reach their ends.
All inputs are finite; a program needn't handle non-finite values.
Results may differ from the reference program's by a relative error of at most 0.024.
Values may be sent and summed in bfloat16 or wider, within the bound.
No kernel may reach another device: no remote copies, remote signals or barrier semaphores. Data moves between devices by JAX's collectives and lax.ppermute only.
A program may use at most 64 MiB of HBM per device.

```python
import jax
import jax.numpy as jnp
from jax import lax

D = 1024
HEADS = 16
HEAD = 64
INNER = 1024
LEVELS = 3
T_DEV = 64
SEQ_LEN = 2048
LAYERS = 16


def shared_query(key):
    draw = jax.random.truncated_normal(key, -4.0, 4.0, (LAYERS, D, INNER), jnp.float32)
    return draw * D ** (-0.5)


def draw_w_query(key, part):
    return shared_query(key).astype(jnp.bfloat16)


def draw_w_key(key, part):
    key = jax.random.fold_in(key, 7)
    own = jax.random.truncated_normal(key, -4.0, 4.0, (LAYERS, D, INNER), jnp.float32) * D ** (-0.5)
    return own.astype(jnp.bfloat16)


def draw_norm_gain(key, part):
    key = jax.random.fold_in(key, 3)
    return jnp.exp(jax.random.uniform(key, (LAYERS, D), jnp.float32, jnp.log(0.5), jnp.log(2.0)))


def steps_of(rng, dims, cuts, smallest, top_value):
    level, own = 1.0, jax.random.fold_in(rng, 6)
    for axis_at, blocks in cuts:
        heights = jnp.exp(jax.random.uniform(jax.random.fold_in(own, axis_at), (blocks,), jnp.float32, smallest / len(cuts), top_value / len(cuts)))
        level = level * jnp.repeat(heights, dims[axis_at] // blocks).reshape([-1 if axis == axis_at else 1 for axis in range(len(dims))])
    return level


def gaussian(key, shape, scale, reach, cuts=(), held_as=jnp.bfloat16):
    drawn = jax.random.normal(key, shape, jnp.float32) * scale
    if len(cuts) > 0:
        drawn = steps_of(key, shape, cuts, -0.22, 0.18) * drawn
    return jnp.clip(drawn, min=-reach, max=reach).astype(held_as)


def setup_inputs(seed: int = 0) -> dict:
    streams_of = jax.random.split(jax.random.key(seed), 9)
    fwd_input = gaussian(streams_of[0], (LAYERS, SEQ_LEN, D), 1.0, 6.0, ((0, 16), (1, 32)))
    bwd_input = gaussian(streams_of[1], (LAYERS, SEQ_LEN, D), 1.0, 6.0, ((0, 16), (1, 32)))
    bwd_grad = gaussian(streams_of[2], (LAYERS, SEQ_LEN, D), 1.0, 6.0, ((0, 16), (1, 32)), jnp.float32)
    norm_gain = draw_norm_gain(jax.random.fold_in(streams_of[8], 71), 0)
    w_query = draw_w_query(jax.random.fold_in(streams_of[8], 71), 0)
    w_key = draw_w_key(jax.random.fold_in(streams_of[8], 71), 0)
    w_value = gaussian(streams_of[6], (LAYERS, D, INNER), D ** -0.5, 0.1875, ((0, 16), (1, 32)))
    w_out = gaussian(streams_of[7], (LAYERS, INNER, D), INNER ** -0.5, 0.1875, ((0, 16), (1, 32)))
    return {"fwd_input": fwd_input, "bwd_input": bwd_input, "bwd_grad": bwd_grad, "norm_gain": norm_gain, "w_query": w_query, "w_key": w_key, "w_value": w_value, "w_out": w_out}


NEG = -1e+30
EPS = 1e-06

def normalize(x, gain):
    xf = x.astype(jnp.float32)
    inv = lax.rsqrt(lax.optimization_barrier(jnp.mean(xf * xf, axis=-1, keepdims=True)) + EPS)
    return ((xf * inv * gain).astype(jnp.bfloat16), xf, inv)

def project(normed, w_query, w_key, w_value):
    shape = (SEQ_LEN, HEADS, HEAD)
    query = jnp.dot(normed, w_query, preferred_element_type=jnp.float32).astype(jnp.bfloat16).reshape(shape)
    keys = jnp.dot(normed, w_key, preferred_element_type=jnp.float32).astype(jnp.bfloat16).reshape(shape)
    values = jnp.dot(normed, w_value, preferred_element_type=jnp.float32).astype(jnp.bfloat16).reshape(shape)
    return (query, keys, values)

def pick(array, level):
    rate = 2 ** level
    offsets = jnp.arange(HEADS) % rate
    shaped = array.reshape((SEQ_LEN // (T_DEV * rate), T_DEV, rate, HEADS) + array.shape[2:])
    return shaped[:, :, offsets, jnp.arange(HEADS)]

def spread(array, level, fill):
    rate = 2 ** level
    hit = jnp.arange(rate)[:, None] == (jnp.arange(HEADS) % rate)[None, :]
    hit = hit.reshape((1, 1, rate, HEADS) + (1,) * (array.ndim - 3))
    full = jnp.where(hit, array[:, :, None], fill)
    return full.reshape((SEQ_LEN, HEADS) + array.shape[3:])

def causal_mask():
    return (jnp.arange(T_DEV)[:, None] >= jnp.arange(T_DEV)[None, :])[None, None]

def level_scores(picked_q, picked_k):
    scores = jnp.einsum('nthe,nuhe->nhtu', picked_q.astype(jnp.float32), picked_k.astype(jnp.float32))
    return scores * HEAD ** (-0.5)

def attend(query, keys, values):
    tops, totals, accums = ([], [], [])
    for level in range(LEVELS):
        picked_q, picked_k, picked_v = (pick(query, level), pick(keys, level), pick(values, level))
        causal = causal_mask()
        scores = jnp.where(causal, level_scores(picked_q, picked_k), NEG)
        top = lax.optimization_barrier(jnp.max(scores, axis=-1))
        weights = jnp.where(causal, jnp.exp(scores - top[..., None]), 0.0)
        total = lax.optimization_barrier(jnp.sum(weights, axis=-1))
        accum = jnp.einsum('nhtu,nuhe->nthe', weights.astype(jnp.bfloat16).astype(jnp.float32), picked_v.astype(jnp.float32))
        tops.append(spread(jnp.swapaxes(top, 1, 2), level, NEG))
        totals.append(spread(jnp.swapaxes(total, 1, 2), level, 0.0))
        accums.append(spread(accum, level, 0.0))
    biggest = tops[0]
    for top in tops[1:]:
        biggest = jnp.maximum(biggest, top)
    denom = jnp.zeros_like(biggest)
    numer = jnp.zeros_like(accums[0])
    for top, total, accum in zip(tops, totals, accums):
        factor = jnp.exp(top - biggest)
        denom = denom + factor * total
        numer = numer + factor[..., None] * accum
    attended = (numer / denom[..., None]).astype(jnp.bfloat16)
    return (attended, biggest + jnp.log(denom))

def forward_layer(x, gain, w_query, w_key, w_value, w_out):
    normed, xf, inv = normalize(x, gain)
    query, keys, values = project(normed, w_query, w_key, w_value)
    attended, lse = attend(query, keys, values)
    mixed = jnp.dot(attended.reshape(SEQ_LEN, INNER), w_out, preferred_element_type=jnp.float32)
    return (xf + mixed).astype(jnp.bfloat16)

def backward_layer(x, grad, gain, w_query, w_key, w_value, w_out):
    normed, xf, inv = normalize(x, gain)
    query, keys, values = project(normed, w_query, w_key, w_value)
    attended, lse = attend(query, keys, values)
    d_att = jnp.dot(grad.astype(jnp.bfloat16), w_out.T, preferred_element_type=jnp.float32).astype(jnp.bfloat16)
    d_att = d_att.reshape(SEQ_LEN, HEADS, HEAD)
    delta = lax.optimization_barrier(jnp.sum(d_att.astype(jnp.float32) * attended.astype(jnp.float32), axis=-1))
    grad_q = jnp.zeros((SEQ_LEN, HEADS, HEAD), jnp.float32)
    grad_k = jnp.zeros((SEQ_LEN, HEADS, HEAD), jnp.float32)
    grad_v = jnp.zeros((SEQ_LEN, HEADS, HEAD), jnp.float32)
    for level in range(LEVELS):
        picked_q, picked_k, picked_v = (pick(query, level), pick(keys, level), pick(values, level))
        picked_d = pick(d_att, level).astype(jnp.float32)
        picked_l = jnp.swapaxes(pick(lse, level), 1, 2)[..., None]
        picked_e = jnp.swapaxes(pick(delta, level), 1, 2)[..., None]
        causal = causal_mask()
        scores = level_scores(picked_q, picked_k)
        prob = jnp.where(causal, jnp.exp(jnp.where(causal, scores, NEG) - picked_l), 0.0)
        dprob = jnp.einsum('nthe,nuhe->nhtu', picked_d, picked_v.astype(jnp.float32))
        dscore = (prob * (dprob - picked_e)).astype(jnp.bfloat16).astype(jnp.float32)
        prob_low = prob.astype(jnp.bfloat16).astype(jnp.float32)
        grad_v = grad_v + spread(jnp.einsum('nhtu,nthe->nuhe', prob_low, picked_d), level, 0.0)
        grad_q = grad_q + spread(jnp.einsum('nhtu,nuhe->nthe', dscore, picked_k.astype(jnp.float32)) * HEAD ** (-0.5), level, 0.0)
        grad_k = grad_k + spread(jnp.einsum('nhtu,nthe->nuhe', dscore, picked_q.astype(jnp.float32)) * HEAD ** (-0.5), level, 0.0)
    shape = (SEQ_LEN, INNER)
    grad_n = jnp.dot(grad_q.astype(jnp.bfloat16).reshape(shape), w_query.T, preferred_element_type=jnp.float32)
    grad_n = grad_n + jnp.dot(grad_k.astype(jnp.bfloat16).reshape(shape), w_key.T, preferred_element_type=jnp.float32)
    grad_n = grad_n + jnp.dot(grad_v.astype(jnp.bfloat16).reshape(shape), w_value.T, preferred_element_type=jnp.float32)
    scaled = grad_n * gain
    nhat = xf * inv
    return grad + inv * (scaled - nhat * lax.optimization_barrier(jnp.mean(scaled * nhat, axis=-1, keepdims=True)))

def reference(fwd_input, bwd_input, bwd_grad, norm_gain, w_query, w_key, w_value, w_out):

    def one_layer(items):
        x_fwd, x_bwd, grad, gain, wq, wk, wv, wo = items
        return (forward_layer(x_fwd, gain, wq, wk, wv, wo), backward_layer(x_bwd, grad, gain, wq, wk, wv, wo))
    outputs, grads = lax.map(one_layer, (fwd_input, bwd_input, bwd_grad, norm_gain, w_query, w_key, w_value, w_out))
    return (jnp.roll(outputs, 1, axis=0), jnp.roll(grads, -1, axis=0))
```

```python
import functools
import math

import jax
import jax.numpy as jnp
from jax import lax
from jax.experimental import pallas as pl
from jax.experimental.pallas import tpu as pltpu
from jax.sharding import PartitionSpec as P

HEAD = 64
EPS = 1e-06
NEG = -1e30
GROUP = 4
HEADS = 4

F32 = jnp.float32
BF16 = jnp.bfloat16
NT = (((1,), (1,)), ((), ()))
NN = (((1,), (0,)), ((), ()))
TN = (((0,), (0,)), ((), ()))


def mm(a, b, dims):
    return lax.dot_general(a, b, dims, preferred_element_type=F32)


def pair_bias(rows):
    t = lax.broadcasted_iota(jnp.int32, (rows, rows), 0)
    u = lax.broadcasted_iota(jnp.int32, (rows, rows), 1)
    causal = u <= t
    apart = t ^ u
    one = causal & (apart < 64)
    two = causal & (apart < 128) & ((apart & 1) == 0)
    three = causal & (apart < 256) & ((apart & 3) == 0)
    biases = []
    for head in range(HEADS):
        count = one.astype(jnp.int32)
        count = count + (two & ((t & 1) == head % 2)).astype(jnp.int32)
        count = count + (three & ((t & 3) == head)).astype(jnp.int32)
        bias = jnp.where(count == 1, 0.0, NEG)
        bias = jnp.where(count == 2, math.log(2.0), bias)
        bias = jnp.where(count == 3, math.log(3.0), bias)
        biases.append(bias)
    return biases


def head_masks(rows):
    lane = lax.broadcasted_iota(jnp.int32, (rows, HEADS * HEAD), 1)
    return [(lane // HEAD) == head for head in range(HEADS)]


def only(mask, value):
    return jnp.where(mask, value, jnp.zeros((), value.dtype))


def pack(q_hbm, k_hbm, v_hbm, o_hbm, fwd_hbm, bwd_hbm, grad_hbm, qkv_out, own_out, tok_out, *scratch):
    grad_ref, sems, more = scratch
    copies = []

    def begin(source, target, sem):
        copies.append(pltpu.make_async_copy(source, target, sem))
        copies[-1].start()

    for block in range(GROUP):
        columns = slice(256 * block, 256 * block + 256)
        for i, ref in enumerate((q_hbm, k_hbm, v_hbm, o_hbm)):
            target = own_out.at[block, 0] if i == 3 else qkv_out.at[block, i]
            begin(ref.at[:, columns], target, sems.at[block, i])
    begin(fwd_hbm, tok_out.at[0], more.at[0])
    begin(bwd_hbm, tok_out.at[1], more.at[1])
    begin(grad_hbm, grad_ref, more.at[2])
    for copy in copies:
        copy.wait()
    tok_out[2] = grad_ref[...].astype(BF16)


def finish(parts_ref, fwd_ref, grad_ref, next_ref, prev_ref):
    for which, own, out in ((0, fwd_ref, next_ref), (1, grad_ref, prev_ref)):
        total = own[...].astype(F32)
        for part in range(GROUP):
            total = total + parts_ref[part, which].astype(F32)
        out[...] = total.astype(BF16)


def layer(me_ref, qkv_hbm, own_hbm, gain_ref, *refs):
    tok_hbm = refs[:GROUP]
    out_hbm, tok_ref, out_ref, w_ref, bias_ref, sems = refs[GROUP:]
    rows = GROUP * 64
    order = {}

    def begin(name, source, target, sem):
        order.setdefault(name, []).append(pltpu.make_async_copy(source, target, sem))
        order[name][-1].start()

    def wait(name):
        for copy in order[name]:
            copy.wait()

    def load_tokens(which, name):
        for k in range(GROUP):
            place = (me_ref[0] + GROUP - k) % GROUP
            begin(name, tok_hbm[k].at[which], tok_ref.at[which, place], sems.at[which, k])

    load_tokens(0, "x")
    begin("q", qkv_hbm.at[:, :, 0], w_ref.at[0], sems.at[3, 0])
    begin("k", qkv_hbm.at[:, :, 1], w_ref.at[1], sems.at[3, 1])
    begin("v", qkv_hbm.at[:, :, 2], w_ref.at[2], sems.at[3, 2])
    begin("o", own_hbm, w_ref.at[3], sems.at[3, 3])
    load_tokens(1, "y")
    load_tokens(2, "g")

    for head, bias in enumerate(pair_bias(rows)):
        bias_ref[head] = bias
    heads = head_masks(rows)
    scale = jnp.asarray(HEAD**-0.5, BF16)

    def weight(i):
        return w_ref[i].reshape(1024, 256)

    def out_weight(c):
        return w_ref[3, :, c].reshape(256, 256)

    def normed_of(which):
        xf = tok_ref[which].reshape(rows, 1024).astype(F32)
        inv = lax.rsqrt(jnp.mean(xf * xf, axis=-1, keepdims=True) + EPS)
        return (xf * inv * gain_ref[...]).astype(BF16), inv

    def prob_of(q_head, k, head):
        s = mm(q_head, k, NT) + bias_ref[head]
        top = jnp.max(s, axis=-1, keepdims=True)
        p = jnp.exp(s - top)
        return p * (1.0 / jnp.sum(p, axis=-1, keepdims=True))

    wait("x")
    normed, _ = normed_of(0)
    wait("q")
    q = mm(normed, weight(0), NN).astype(BF16) * scale
    wait("k")
    k = mm(normed, weight(1), NN).astype(BF16)
    wait("v")
    v = mm(normed, weight(2), NN).astype(BF16)
    attended = jnp.zeros((rows, 256), F32)
    for head in range(HEADS):
        p = prob_of(only(heads[head], q), k, head).astype(BF16)
        attended = attended + mm(p, only(heads[head], v), NN)
    attended = attended.astype(BF16)
    wait("o")
    for c in range(4):
        part = mm(attended, out_weight(c), NN).astype(BF16)
        for to in range(GROUP):
            out_ref[to, 0, :, 256 * c : 256 * c + 256] = part[64 * to : 64 * to + 64]
    begin("out", out_ref.at[:, 0], out_hbm.at[:, 0], sems.at[4, 0])

    wait("y")
    normed, inv = normed_of(1)
    q, k, v = [mm(normed, weight(i), NN).astype(BF16) for i in range(3)]
    q = q * scale
    wait("g")
    grads = tok_ref[2].reshape(rows, 1024)
    d_att = jnp.zeros((rows, 256), F32)
    for c in range(4):
        d_att = d_att + mm(grads[:, 256 * c : 256 * c + 256], out_weight(c), NT)
    d_att = d_att.astype(BF16)
    dq = jnp.zeros((rows, 256), F32)
    dk = jnp.zeros((rows, 256), F32)
    dv = jnp.zeros((rows, 256), F32)
    for head in range(HEADS):
        mask = heads[head]
        q_head = only(mask, q)
        p = prob_of(q_head, k, head)
        d_head = only(mask, d_att)
        dp = mm(d_head, v, NT)
        delta = jnp.sum(p * dp, axis=-1, keepdims=True)
        ds = (p * (dp - delta)).astype(BF16)
        dq = dq + mm(ds, only(mask, k), NN)
        dk = dk + mm(ds, q_head, TN)
        dv = dv + mm(p.astype(BF16), d_head, TN)
    dq = (dq * HEAD**-0.5).astype(BF16)
    dk = dk.astype(BF16)
    dv = dv.astype(BF16)
    dn = mm(dq, weight(0), NT) + mm(dk, weight(1), NT) + mm(dv, weight(2), NT)
    for to in range(GROUP):
        part = slice(64 * to, 64 * to + 64)
        scaled = dn[part] * gain_ref[...]
        nhat = tok_ref[1, to].astype(F32) * inv[part]
        dx = inv[part] * (scaled - nhat * jnp.mean(scaled * nhat, axis=-1, keepdims=True))
        out_ref[to, 1] = dx.astype(BF16)
    begin("out", out_ref.at[:, 1], out_hbm.at[:, 1], sems.at[4, 1])
    wait("out")


VMEM = pl.BlockSpec(memory_space=pltpu.VMEM)
HBM = pl.BlockSpec(memory_space=pltpu.HBM)
SMEM = pl.BlockSpec(memory_space=pltpu.SMEM)


def call(body, shapes, inputs, name, in_specs=None, scratch=(), flops=10**6, mib=40, out=VMEM):
    return pl.pallas_call(
        body,
        out_shape=[jax.ShapeDtypeStruct(shape, kind) for shape, kind in shapes],
        in_specs=[VMEM] * len(inputs) if in_specs is None else in_specs,
        out_specs=[out] * len(shapes),
        scratch_shapes=list(scratch),
        compiler_params=pltpu.CompilerParams(vmem_limit_bytes=mib * 2**20),
        cost_estimate=pl.CostEstimate(flops=flops, bytes_accessed=10**6, transcendentals=0),
        name=name,
    )(*inputs)


def per_device(fwd_input, bwd_input, bwd_grad, norm_gain, w_query, w_key, w_value, w_out):
    seqs = lax.axis_size("seq")
    sections = lax.axis_size("section")
    deep = seqs // GROUP
    row_groups = [[GROUP * y + x for x in range(GROUP)] for y in range(deep)]
    columns = [[GROUP * y + x for y in range(deep)] for x in range(GROUP)]
    me = (lax.axis_index("seq") % GROUP).reshape(1)

    qkv, own, tokens = call(
        pack,
        [((GROUP, 3, 32, 256), BF16), ((GROUP, 1, 32, 256), BF16), ((3, 64, 1024), BF16)],
        (w_query[0], w_key[0], w_value[0], w_out[0], fwd_input[0], bwd_input[0], bwd_grad[0]),
        "pack",
        in_specs=[HBM] * 7,
        scratch=(
            pltpu.VMEM((64, 1024), F32),
            pltpu.SemaphoreType.DMA((GROUP, 4)),
            pltpu.SemaphoreType.DMA((3,)),
        ),
        mib=62,
    )
    qkv = lax.all_to_all(qkv, "seq", 0, 0, axis_index_groups=row_groups, tiled=True)
    own = lax.ppermute(own, "seq", [(s, GROUP * (s % deep) + s // deep) for s in range(seqs)])

    qkv, tokens = lax.optimization_barrier((qkv, tokens))
    qkv = lax.all_gather(qkv, "seq", axis_index_groups=columns)
    own = jnp.broadcast_to(own.reshape(1, GROUP, 32, 256), (deep, GROUP, 32, 256))
    own = lax.all_to_all(own, "seq", 0, 0, axis_index_groups=columns, tiled=True)

    all_tokens = [tokens]
    for step in range(1, GROUP):
        pairs = [(s, s - s % GROUP + (s + step) % GROUP) for s in range(seqs)]
        all_tokens.append(lax.ppermute(tokens, "seq", pairs))
    parts, = call(
        layer,
        [((GROUP, 2, 64, 1024), BF16)],
        (me, qkv, own, norm_gain, *all_tokens),
        "layer",
        in_specs=[SMEM, HBM, HBM, VMEM] + [HBM] * GROUP,
        scratch=(
            pltpu.VMEM((3, GROUP, 64, 1024), BF16),
            pltpu.VMEM((GROUP, 2, 64, 1024), BF16),
            pltpu.VMEM((4, deep, GROUP, 32, 256), BF16),
            pltpu.VMEM((HEADS, 256, 256), F32),
            pltpu.SemaphoreType.DMA((5, 4)),
        ),
        flops=15 * 10**8,
        mib=60,
        out=HBM,
    )
    parts = lax.all_to_all(parts, "seq", 0, 0, axis_index_groups=row_groups, tiled=True)
    layer_out, input_grad = call(
        finish,
        [((64, 1024), BF16)] * 2,
        (parts, fwd_input[0], bwd_grad[0]),
        "finish",
    )
    ring = [(c, (c + 1) % sections) for c in range(sections)]
    next_input = lax.ppermute(layer_out, "section", ring)
    prev_grad = lax.ppermute(input_grad, "section", [(b, a) for a, b in ring])
    return next_input[None], prev_grad.astype(F32)[None]


def solution(mesh):
    placed = (
        P("section", "seq", None),
        P("section", "seq", None),
        P("section", "seq", None),
        P("section", None),
        P("section", "seq", None),
        P("section", "seq", None),
        P("section", "seq", None),
        P("section", "seq", None),
    )
    return jax.shard_map(
        per_device,
        mesh=mesh,
        in_specs=placed,
        out_specs=(P("section", "seq", None), P("section", "seq", None)),
        check_vma=False,
    )
```

```python
import functools
import math

import jax
import jax.numpy as jnp
from jax import lax
from jax.experimental import pallas as pl
from jax.experimental.pallas import tpu as pltpu
from jax.sharding import PartitionSpec as P

HEAD = 64
EPS = 1e-06
NEG = -1e30
GROUP = 4
HEADS = 4

F32 = jnp.float32
BF16 = jnp.bfloat16
NT = (((1,), (1,)), ((), ()))
NN = (((1,), (0,)), ((), ()))
TN = (((0,), (0,)), ((), ()))


def mm(a, b, dims):
    return lax.dot_general(a, b, dims, preferred_element_type=F32)


def pair_bias(rows):
    t = lax.broadcasted_iota(jnp.int32, (rows, rows), 0)
    u = lax.broadcasted_iota(jnp.int32, (rows, rows), 1)
    causal = u <= t
    apart = t ^ u
    one = causal & (apart < 64)
    two = causal & (apart < 128) & ((apart & 1) == 0)
    three = causal & (apart < 256) & ((apart & 3) == 0)
    biases = []
    for head in range(HEADS):
        count = one.astype(jnp.int32)
        count = count + (two & ((t & 1) == head % 2)).astype(jnp.int32)
        count = count + (three & ((t & 3) == head)).astype(jnp.int32)
        bias = jnp.where(count == 1, 0.0, NEG)
        bias = jnp.where(count == 2, math.log(2.0), bias)
        bias = jnp.where(count == 3, math.log(3.0), bias)
        biases.append(bias)
    return biases


def head_masks(rows):
    lane = lax.broadcasted_iota(jnp.int32, (rows, HEADS * HEAD), 1)
    return [(lane // HEAD) == head for head in range(HEADS)]


def only(mask, value):
    return jnp.where(mask, value, jnp.zeros((), value.dtype))


def pack_weights(q_hbm, k_hbm, v_hbm, o_hbm, qkv_out, own_out, sems):
    copies = []
    for block in range(GROUP):
        columns = slice(256 * block, 256 * block + 256)
        for i, ref in enumerate((q_hbm, k_hbm, v_hbm, o_hbm)):
            target = own_out.at[block, 0] if i == 3 else qkv_out.at[block, i]
            copies.append(pltpu.make_async_copy(ref.at[:, columns], target, sems.at[block, i]))
            copies[-1].start()
    for copy in copies:
        copy.wait()


def pack_tokens(fwd_hbm, bwd_hbm, grad_hbm, out_ref, grad_ref, sems, grad_sem):
    first = pltpu.make_async_copy(grad_hbm, grad_ref, grad_sem)
    first.start()
    copies = []
    for to in range(GROUP):
        for i, ref in enumerate((fwd_hbm, bwd_hbm)):
            copies.append(pltpu.make_async_copy(ref, out_ref.at[to, i], sems.at[to, i]))
            copies[-1].start()
    first.wait()
    for to in range(GROUP):
        out_ref[to, 2] = grad_ref[...].astype(BF16)
    for copy in copies:
        copy.wait()


def finish(parts_ref, fwd_ref, grad_ref, next_ref, prev_ref):
    for which, own, out in ((0, fwd_ref, next_ref), (1, grad_ref, prev_ref)):
        total = own[...].astype(F32)
        for part in range(GROUP):
            total = total + parts_ref[part, which].astype(F32)
        out[...] = total.astype(BF16)


def prepare(tok_ref, gain_ref, normed_ref, inv_ref, bias_ref):
    for which in range(2):
        for part in range(GROUP):
            xf = tok_ref[part, which].astype(F32)
            inv = lax.rsqrt(jnp.mean(xf * xf, axis=-1, keepdims=True) + EPS)
            rows = slice(64 * part, 64 * part + 64)
            normed_ref[which, rows, :] = (xf * inv * gain_ref[...]).astype(BF16)
            if which == 1:
                inv_ref[rows, :] = jnp.broadcast_to(inv, (64, 128))
    for head, bias in enumerate(pair_bias(GROUP * 64)):
        bias_ref[head] = bias


def layer(row_ref, tok_ref, normed_ref, inv_ref, bias_ref, gain_ref, qkv_ref, *refs):
    pieces, (out_ref, own_ref) = refs[:-2], refs[-2:]
    rows = GROUP * 64
    deep = 2 * len(pieces)
    for k in range(deep):
        own_ref[(row_ref[0] + k) % deep] = pieces[k // 2][k % 2]
    heads = head_masks(rows)
    scale = jnp.asarray(HEAD**-0.5, BF16)

    def weight(i):
        return qkv_ref[:, :, i].reshape(1024, 256)

    def out_weight(c):
        return own_ref[:, c].reshape(256, 256)

    def projected(which):
        normed = normed_ref[which]
        q, k, v = [mm(normed, weight(i), NN).astype(BF16) for i in range(3)]
        return q * scale, k, v

    def prob_of(q_head, k, head):
        s = mm(q_head, k, NT) + bias_ref[head]
        top = jnp.max(s, axis=-1, keepdims=True)
        p = jnp.exp(s - top)
        return p * (1.0 / jnp.sum(p, axis=-1, keepdims=True))

    q, k, v = projected(0)
    attended = jnp.zeros((rows, 256), F32)
    for head in range(HEADS):
        p = prob_of(only(heads[head], q), k, head).astype(BF16)
        attended = attended + mm(p, only(heads[head], v), NN)
    attended = attended.astype(BF16)
    for c in range(4):
        part = mm(attended, out_weight(c), NN).astype(BF16)
        for to in range(GROUP):
            out_ref[to, 0, :, 256 * c : 256 * c + 256] = part[64 * to : 64 * to + 64]

    q, k, v = projected(1)
    grads = tok_ref[:, 2].reshape(rows, 1024)
    d_att = jnp.zeros((rows, 256), F32)
    for c in range(4):
        d_att = d_att + mm(grads[:, 256 * c : 256 * c + 256], out_weight(c), NT)
    d_att = d_att.astype(BF16)
    dq = jnp.zeros((rows, 256), F32)
    dk = jnp.zeros((rows, 256), F32)
    dv = jnp.zeros((rows, 256), F32)
    for head in range(HEADS):
        mask = heads[head]
        q_head = only(mask, q)
        p = prob_of(q_head, k, head)
        d_head = only(mask, d_att)
        dp = mm(d_head, v, NT)
        delta = jnp.sum(p * dp, axis=-1, keepdims=True)
        ds = (p * (dp - delta)).astype(BF16)
        dq = dq + mm(ds, only(mask, k), NN)
        dk = dk + mm(ds, q_head, TN)
        dv = dv + mm(p.astype(BF16), d_head, TN)
    dq = (dq * HEAD**-0.5).astype(BF16)
    dk = dk.astype(BF16)
    dv = dv.astype(BF16)
    dn = mm(dq, weight(0), NT) + mm(dk, weight(1), NT) + mm(dv, weight(2), NT)
    for to in range(GROUP):
        part = slice(64 * to, 64 * to + 64)
        inv = inv_ref[part, 0:1]
        scaled = dn[part] * gain_ref[...]
        nhat = tok_ref[to, 1].astype(F32) * inv
        dx = inv * (scaled - nhat * jnp.mean(scaled * nhat, axis=-1, keepdims=True))
        out_ref[to, 1] = dx.astype(BF16)


VMEM = pl.BlockSpec(memory_space=pltpu.VMEM)
HBM = pl.BlockSpec(memory_space=pltpu.HBM)
SMEM = pl.BlockSpec(memory_space=pltpu.SMEM)


def call(body, shapes, inputs, name, in_specs=None, scratch=(), flops=10**6, mib=40, out=VMEM):
    return pl.pallas_call(
        body,
        out_shape=[jax.ShapeDtypeStruct(shape, kind) for shape, kind in shapes],
        in_specs=[VMEM] * len(inputs) if in_specs is None else in_specs,
        out_specs=[out] * len(shapes),
        scratch_shapes=list(scratch),
        compiler_params=pltpu.CompilerParams(vmem_limit_bytes=mib * 2**20),
        cost_estimate=pl.CostEstimate(flops=flops, bytes_accessed=10**6, transcendentals=0),
        name=name,
    )(*inputs)


def per_device(fwd_input, bwd_input, bwd_grad, norm_gain, w_query, w_key, w_value, w_out):
    seqs = lax.axis_size("seq")
    sections = lax.axis_size("section")
    deep = seqs // GROUP
    row_groups = [[GROUP * y + x for x in range(GROUP)] for y in range(deep)]
    columns = [[GROUP * y + x for y in range(deep)] for x in range(GROUP)]
    row = (lax.axis_index("seq") // GROUP).reshape(1)

    qkv, own = call(
        pack_weights,
        [((GROUP, 3, 32, 256), BF16), ((GROUP, 1, 32, 256), BF16)],
        (w_query[0], w_key[0], w_value[0], w_out[0]),
        "pack_weights",
        in_specs=[HBM] * 4,
        scratch=(pltpu.SemaphoreType.DMA((GROUP, 4)),),
        mib=63,
    )
    qkv = lax.all_to_all(qkv, "seq", 0, 0, axis_index_groups=row_groups, tiled=True)
    own = lax.ppermute(own, "seq", [(s, GROUP * (s % deep) + s // deep) for s in range(seqs)])
    tokens, = call(
        pack_tokens,
        [((GROUP, 3, 64, 1024), BF16)],
        (fwd_input[0], bwd_input[0], bwd_grad[0]),
        "pack_tokens",
        in_specs=[HBM] * 3,
        scratch=(
            pltpu.VMEM((64, 1024), F32),
            pltpu.SemaphoreType.DMA((GROUP, 2)),
            pltpu.SemaphoreType.DMA,
        ),
        mib=63,
    )
    mine = qkv
    qkv = lax.all_gather(qkv, "seq", axis_index_groups=columns)
    _, own, tokens = lax.optimization_barrier((mine, own, tokens))
    tokens = lax.all_to_all(tokens, "seq", 0, 0, axis_index_groups=row_groups, tiled=True)
    def up(value, steps):
        return lax.ppermute(
            value, "seq", [(s, (s - steps * GROUP) % seqs) for s in range(seqs)]
        )

    own = own.reshape(1, GROUP, 32, 256)
    pieces = [jnp.concatenate((own, up(own, 1)))]
    for step in range(2, deep, 2):
        pieces.append(up(pieces[-1], 2))
        if step == 4:
            pieces[-1], tokens = lax.optimization_barrier((pieces[-1], tokens))

    normed, inv, bias = call(
        prepare,
        [((2, 256, 1024), BF16), ((256, 128), F32), ((HEADS, 256, 256), F32)],
        (tokens, norm_gain),
        "prepare",
    )
    parts, = call(
        layer,
        [((GROUP, 2, 64, 1024), BF16)],
        (row, tokens, normed, inv, bias, norm_gain, qkv, *pieces),
        "layer",
        in_specs=[SMEM] + [VMEM] * (6 + deep // 2),
        scratch=(pltpu.VMEM((deep, GROUP, 32, 256), BF16),),
        flops=15 * 10**8,
    )
    parts = lax.all_to_all(parts, "seq", 0, 0, axis_index_groups=row_groups, tiled=True)
    layer_out, input_grad = call(
        finish,
        [((64, 1024), BF16)] * 2,
        (parts, fwd_input[0], bwd_grad[0]),
        "finish",
    )
    ring = [(c, (c + 1) % sections) for c in range(sections)]
    next_input = lax.ppermute(layer_out, "section", ring)
    prev_grad = lax.ppermute(input_grad, "section", [(b, a) for a, b in ring])
    return next_input[None], prev_grad.astype(F32)[None]


def solution(mesh):
    placed = (
        P("section", "seq", None),
        P("section", "seq", None),
        P("section", "seq", None),
        P("section", None),
        P("section", "seq", None),
        P("section", "seq", None),
        P("section", "seq", None),
        P("section", "seq", None),
    )
    return jax.shard_map(
        per_device,
        mesh=mesh,
        in_specs=placed,
        out_specs=(P("section", "seq", None), P("section", "seq", None)),
        check_vma=False,
    )
```

```python
import functools
import math

import jax
import jax.numpy as jnp
from jax import lax
from jax.experimental import pallas as pl
from jax.experimental.pallas import tpu as pltpu
from jax.sharding import PartitionSpec as P

HEAD = 64
EPS = 1e-06
NEG = -1e30
GROUP = 4
HEADS = 4

F32 = jnp.float32
BF16 = jnp.bfloat16
NT = (((1,), (1,)), ((), ()))
NN = (((1,), (0,)), ((), ()))
TN = (((0,), (0,)), ((), ()))


def mm(a, b, dims):
    return lax.dot_general(a, b, dims, preferred_element_type=F32)


def pair_bias(rows):
    t = lax.broadcasted_iota(jnp.int32, (rows, rows), 0)
    u = lax.broadcasted_iota(jnp.int32, (rows, rows), 1)
    causal = u <= t
    apart = t ^ u
    one = causal & (apart < 64)
    two = causal & (apart < 128) & ((apart & 1) == 0)
    three = causal & (apart < 256) & ((apart & 3) == 0)
    biases = []
    for head in range(HEADS):
        count = one.astype(jnp.int32)
        count = count + (two & ((t & 1) == head % 2)).astype(jnp.int32)
        count = count + (three & ((t & 3) == head)).astype(jnp.int32)
        bias = jnp.where(count == 1, 0.0, NEG)
        bias = jnp.where(count == 2, math.log(2.0), bias)
        bias = jnp.where(count == 3, math.log(3.0), bias)
        biases.append(bias)
    return biases


def head_masks(rows):
    lane = lax.broadcasted_iota(jnp.int32, (rows, HEADS * HEAD), 1)
    return [(lane // HEAD) == head for head in range(HEADS)]


def only(mask, value):
    return jnp.where(mask, value, jnp.zeros((), value.dtype))


def pack_weights(q_hbm, k_hbm, v_hbm, o_hbm, qkv_out, own_out, sems):
    copies = []
    for block in range(GROUP):
        columns = slice(256 * block, 256 * block + 256)
        for i, ref in enumerate((q_hbm, k_hbm, v_hbm, o_hbm)):
            target = own_out.at[block, 0] if i == 3 else qkv_out.at[block, i]
            copies.append(pltpu.make_async_copy(ref.at[:, columns], target, sems.at[block, i]))
            copies[-1].start()
    for copy in copies:
        copy.wait()


def pack_tokens(fwd_hbm, bwd_hbm, grad_hbm, out_ref, grad_ref, sems, grad_sem):
    first = pltpu.make_async_copy(grad_hbm, grad_ref, grad_sem)
    first.start()
    copies = []
    for to in range(GROUP):
        for i, ref in enumerate((fwd_hbm, bwd_hbm)):
            copies.append(pltpu.make_async_copy(ref, out_ref.at[to, i], sems.at[to, i]))
            copies[-1].start()
    first.wait()
    for to in range(GROUP):
        out_ref[to, 2] = grad_ref[...].astype(BF16)
    for copy in copies:
        copy.wait()


def finish(parts_ref, fwd_ref, grad_ref, next_ref, prev_ref):
    for which, own, out in ((0, fwd_ref, next_ref), (1, grad_ref, prev_ref)):
        total = own[...].astype(F32)
        for part in range(GROUP):
            total = total + parts_ref[part, which].astype(F32)
        out[...] = total.astype(BF16)


def prepare(tok_ref, gain_ref, normed_ref, inv_ref):
    for which in range(2):
        for part in range(GROUP):
            xf = tok_ref[part, which].astype(F32)
            inv = lax.rsqrt(jnp.mean(xf * xf, axis=-1, keepdims=True) + EPS)
            rows = slice(64 * part, 64 * part + 64)
            normed_ref[which, rows, :] = (xf * inv * gain_ref[...]).astype(BF16)
            if which == 1:
                inv_ref[rows, :] = jnp.broadcast_to(inv, (64, 128))


def deliver(next_ref, prev_ref, next_out, prev_out):
    next_out[...] = next_ref[...]
    prev_out[...] = prev_ref[...].astype(F32)


def layer(tok_ref, normed_ref, inv_ref, gain_ref, w_ref, out_ref, bias_ref):
    rows = GROUP * 64
    for head, bias in enumerate(pair_bias(rows)):
        bias_ref[head] = bias
    heads = head_masks(rows)
    scale = jnp.asarray(HEAD**-0.5, BF16)

    def weight(i):
        return w_ref[:, :, i].reshape(1024, 256)

    def out_weight(c):
        return w_ref[:, c, 3].reshape(256, 256)

    def projected(which):
        normed = normed_ref[which]
        q, k, v = [mm(normed, weight(i), NN).astype(BF16) for i in range(3)]
        return q * scale, k, v

    def prob_of(q_head, k, head):
        s = mm(q_head, k, NT) + bias_ref[head]
        top = jnp.max(s, axis=-1, keepdims=True)
        p = jnp.exp(s - top)
        return p * (1.0 / jnp.sum(p, axis=-1, keepdims=True))

    q, k, v = projected(0)
    attended = jnp.zeros((rows, 256), F32)
    for head in range(HEADS):
        p = prob_of(only(heads[head], q), k, head).astype(BF16)
        attended = attended + mm(p, only(heads[head], v), NN)
    attended = attended.astype(BF16)
    for c in range(4):
        part = mm(attended, out_weight(c), NN).astype(BF16)
        for to in range(GROUP):
            out_ref[to, 0, :, 256 * c : 256 * c + 256] = part[64 * to : 64 * to + 64]

    q, k, v = projected(1)
    grads = tok_ref[:, 2].reshape(rows, 1024)
    d_att = jnp.zeros((rows, 256), F32)
    for c in range(4):
        d_att = d_att + mm(grads[:, 256 * c : 256 * c + 256], out_weight(c), NT)
    d_att = d_att.astype(BF16)
    dq = jnp.zeros((rows, 256), F32)
    dk = jnp.zeros((rows, 256), F32)
    dv = jnp.zeros((rows, 256), F32)
    for head in range(HEADS):
        mask = heads[head]
        q_head = only(mask, q)
        p = prob_of(q_head, k, head)
        d_head = only(mask, d_att)
        dp = mm(d_head, v, NT)
        delta = jnp.sum(p * dp, axis=-1, keepdims=True)
        ds = (p * (dp - delta)).astype(BF16)
        dq = dq + mm(ds, only(mask, k), NN)
        dk = dk + mm(ds, q_head, TN)
        dv = dv + mm(p.astype(BF16), d_head, TN)
    dq = (dq * HEAD**-0.5).astype(BF16)
    dk = dk.astype(BF16)
    dv = dv.astype(BF16)
    dn = mm(dq, weight(0), NT) + mm(dk, weight(1), NT) + mm(dv, weight(2), NT)
    for to in range(GROUP):
        part = slice(64 * to, 64 * to + 64)
        inv = inv_ref[part, 0:1]
        scaled = dn[part] * gain_ref[...]
        nhat = tok_ref[to, 1].astype(F32) * inv
        dx = inv * (scaled - nhat * jnp.mean(scaled * nhat, axis=-1, keepdims=True))
        out_ref[to, 1] = dx.astype(BF16)


VMEM = pl.BlockSpec(memory_space=pltpu.VMEM)
HBM = pl.BlockSpec(memory_space=pltpu.HBM)
SMEM = pl.BlockSpec(memory_space=pltpu.SMEM)


def call(body, shapes, inputs, name, in_specs=None, scratch=(), flops=10**6, mib=40, out=VMEM):
    return pl.pallas_call(
        body,
        out_shape=[jax.ShapeDtypeStruct(shape, kind) for shape, kind in shapes],
        in_specs=[VMEM] * len(inputs) if in_specs is None else in_specs,
        out_specs=[out] * len(shapes),
        scratch_shapes=list(scratch),
        compiler_params=pltpu.CompilerParams(vmem_limit_bytes=mib * 2**20),
        cost_estimate=pl.CostEstimate(flops=flops, bytes_accessed=10**6, transcendentals=0),
        name=name,
    )(*inputs)


def per_device(fwd_input, bwd_input, bwd_grad, norm_gain, w_query, w_key, w_value, w_out):
    seqs = lax.axis_size("seq")
    sections = lax.axis_size("section")
    deep = seqs // GROUP
    row_groups = [[GROUP * y + x for x in range(GROUP)] for y in range(deep)]
    columns = [[GROUP * y + x for y in range(deep)] for x in range(GROUP)]

    qkv, own = call(
        pack_weights,
        [((GROUP, 3, 32, 256), BF16), ((GROUP, 1, 32, 256), BF16)],
        (w_query[0], w_key[0], w_value[0], w_out[0]),
        "pack_weights",
        in_specs=[HBM] * 4,
        scratch=(pltpu.SemaphoreType.DMA((GROUP, 4)),),
        mib=63,
    )
    qkv = lax.all_to_all(qkv, "seq", 0, 0, axis_index_groups=row_groups, tiled=True)
    own = lax.ppermute(own, "seq", [(s, GROUP * (s % deep) + s // deep) for s in range(seqs)])
    tokens, = call(
        pack_tokens,
        [((GROUP, 3, 64, 1024), BF16)],
        (fwd_input[0], bwd_input[0], bwd_grad[0]),
        "pack_tokens",
        in_specs=[HBM] * 3,
        scratch=(
            pltpu.VMEM((64, 1024), F32),
            pltpu.SemaphoreType.DMA((GROUP, 2)),
            pltpu.SemaphoreType.DMA,
        ),
        mib=63,
    )
    weights = jnp.concatenate((qkv, own), axis=1)
    weights, tokens = lax.optimization_barrier((weights, tokens))
    weights = lax.all_gather(weights, "seq", axis_index_groups=columns)
    tokens = lax.all_to_all(tokens, "seq", 0, 0, axis_index_groups=row_groups, tiled=True)
    normed, inv = call(
        prepare,
        [((2, 256, 1024), BF16), ((256, 128), F32)],
        (tokens, norm_gain),
        "prepare",
    )
    parts, = call(
        layer,
        [((GROUP, 2, 64, 1024), BF16)],
        (tokens, normed, inv, norm_gain, weights),
        "layer",
        scratch=(pltpu.VMEM((HEADS, 256, 256), F32),),
        flops=15 * 10**8,
    )
    parts = lax.all_to_all(parts, "seq", 0, 0, axis_index_groups=row_groups, tiled=True)
    layer_out, input_grad = call(
        finish,
        [((64, 1024), BF16)] * 2,
        (parts, fwd_input[0], bwd_grad[0]),
        "finish",
    )
    ring = [(c, (c + 1) % sections) for c in range(sections)]
    next_input = lax.ppermute(layer_out, "section", ring)
    prev_grad = lax.ppermute(input_grad, "section", [(b, a) for a, b in ring])
    next_input, prev_grad = call(
        deliver,
        [((64, 1024), BF16), ((64, 1024), F32)],
        (next_input, prev_grad),
        "deliver",
    )
    return next_input[None], prev_grad[None]


def solution(mesh):
    placed = (
        P("section", "seq", None),
        P("section", "seq", None),
        P("section", "seq", None),
        P("section", None),
        P("section", "seq", None),
        P("section", "seq", None),
        P("section", "seq", None),
        P("section", "seq", None),
    )
    return jax.shard_map(
        per_device,
        mesh=mesh,
        in_specs=placed,
        out_specs=(P("section", "seq", None), P("section", "seq", None)),
        check_vma=False,
    )
```

```python
import functools
import math

import jax
import jax.numpy as jnp
from jax import lax
from jax.experimental import pallas as pl
from jax.experimental.pallas import tpu as pltpu
from jax.sharding import PartitionSpec as P

HEAD = 64
EPS = 1e-06
NEG = -1e30
GROUP = 4
HEADS = 4

F32 = jnp.float32
BF16 = jnp.bfloat16
NT = (((1,), (1,)), ((), ()))
NN = (((1,), (0,)), ((), ()))
TN = (((0,), (0,)), ((), ()))


def mm(a, b, dims):
    return lax.dot_general(a, b, dims, preferred_element_type=F32)


def pair_bias(rows):
    t = lax.broadcasted_iota(jnp.int32, (rows, rows), 0)
    u = lax.broadcasted_iota(jnp.int32, (rows, rows), 1)
    causal = u <= t
    apart = t ^ u
    one = causal & (apart < 64)
    two = causal & (apart < 128) & ((apart & 1) == 0)
    three = causal & (apart < 256) & ((apart & 3) == 0)
    biases = []
    for head in range(HEADS):
        count = one.astype(jnp.int32)
        count = count + (two & ((t & 1) == head % 2)).astype(jnp.int32)
        count = count + (three & ((t & 3) == head)).astype(jnp.int32)
        bias = jnp.where(count == 1, 0.0, NEG)
        bias = jnp.where(count == 2, math.log(2.0), bias)
        bias = jnp.where(count == 3, math.log(3.0), bias)
        biases.append(bias)
    return biases


def head_masks(rows):
    lane = lax.broadcasted_iota(jnp.int32, (rows, HEADS * HEAD), 1)
    return [(lane // HEAD) == head for head in range(HEADS)]


def only(mask, value):
    return jnp.where(mask, value, jnp.zeros((), value.dtype))


def pack_weights(q_hbm, k_hbm, v_hbm, out_ref, sems):
    copies = []
    for block in range(GROUP):
        columns = slice(256 * block, 256 * block + 256)
        for i, ref in enumerate((q_hbm, k_hbm, v_hbm)):
            source, target = ref.at[:, columns], out_ref.at[block, i]
            copies.append(pltpu.make_async_copy(source, target, sems.at[block, i]))
            copies[-1].start()
    for copy in copies:
        copy.wait()


def join_weights(qkv_ref, own_ref, out_ref):
    for block in range(GROUP):
        out_ref[block, :3] = qkv_ref[block]
        out_ref[block, 3] = own_ref[:, 256 * block : 256 * block + 256]


def pack_tokens(after_hbm, fwd_hbm, bwd_hbm, grad_hbm, out_ref, grad_ref, sems, grad_sem):
    del after_hbm
    first = pltpu.make_async_copy(grad_hbm, grad_ref, grad_sem)
    first.start()
    copies = []
    for to in range(GROUP):
        for i, ref in enumerate((fwd_hbm, bwd_hbm)):
            copies.append(pltpu.make_async_copy(ref, out_ref.at[to, i], sems.at[to, i]))
            copies[-1].start()
    first.wait()
    for to in range(GROUP):
        out_ref[to, 2] = grad_ref[...].astype(BF16)
    for copy in copies:
        copy.wait()


def finish(parts_ref, fwd_ref, grad_ref, next_ref, prev_ref):
    for which, own, out in ((0, fwd_ref, next_ref), (1, grad_ref, prev_ref)):
        total = own[...].astype(F32)
        for part in range(GROUP):
            total = total + parts_ref[part, which].astype(F32)
        out[...] = total.astype(BF16)


def prepare(tok_ref, gain_ref, normed_ref, inv_ref, bias_ref):
    for which in range(2):
        for part in range(GROUP):
            xf = tok_ref[part, which].astype(F32)
            inv = lax.rsqrt(jnp.mean(xf * xf, axis=-1, keepdims=True) + EPS)
            rows = slice(64 * part, 64 * part + 64)
            normed_ref[which, rows, :] = (xf * inv * gain_ref[...]).astype(BF16)
            if which == 1:
                inv_ref[rows, :] = jnp.broadcast_to(inv, (64, 128))
    for head, bias in enumerate(pair_bias(GROUP * 64)):
        bias_ref[head] = bias


def deliver(next_ref, prev_ref, next_out, prev_out):
    next_out[...] = next_ref[...]
    prev_out[...] = prev_ref[...].astype(F32)


def layer(tok_ref, normed_ref, inv_ref, bias_ref, gain_ref, w_hbm, out_ref, w_ref, sems):
    rows = GROUP * 64
    copies = []
    for i in range(4):
        copies.append(pltpu.make_async_copy(w_hbm.at[:, :, i], w_ref.at[i], sems.at[i]))
        copies[-1].start()
    heads = head_masks(rows)
    scale = jnp.asarray(HEAD**-0.5, BF16)

    def weight(i):
        return w_ref[i].reshape(1024, 256)

    def out_weight(c):
        return w_ref[3, :, c].reshape(256, 256)

    def projected(which):
        results = []
        for i in range(3):
            if which == 0:
                copies[i].wait()
            results.append(mm(normed_ref[which], weight(i), NN).astype(BF16))
        q, k, v = results
        return q * scale, k, v

    def prob_of(q_head, k, head):
        s = mm(q_head, k, NT) + bias_ref[head]
        top = jnp.max(s, axis=-1, keepdims=True)
        p = jnp.exp(s - top)
        return p * (1.0 / jnp.sum(p, axis=-1, keepdims=True))

    q, k, v = projected(0)
    attended = jnp.zeros((rows, 256), F32)
    for head in range(HEADS):
        p = prob_of(only(heads[head], q), k, head).astype(BF16)
        attended = attended + mm(p, only(heads[head], v), NN)
    attended = attended.astype(BF16)
    copies[3].wait()
    for c in range(4):
        part = mm(attended, out_weight(c), NN).astype(BF16)
        for to in range(GROUP):
            out_ref[to, 0, :, 256 * c : 256 * c + 256] = part[64 * to : 64 * to + 64]

    q, k, v = projected(1)
    grads = tok_ref[:, 2].reshape(rows, 1024)
    d_att = jnp.zeros((rows, 256), F32)
    for c in range(4):
        d_att = d_att + mm(grads[:, 256 * c : 256 * c + 256], out_weight(c), NT)
    d_att = d_att.astype(BF16)
    dq = jnp.zeros((rows, 256), F32)
    dk = jnp.zeros((rows, 256), F32)
    dv = jnp.zeros((rows, 256), F32)
    for head in range(HEADS):
        mask = heads[head]
        q_head = only(mask, q)
        p = prob_of(q_head, k, head)
        d_head = only(mask, d_att)
        dp = mm(d_head, v, NT)
        delta = jnp.sum(p * dp, axis=-1, keepdims=True)
        ds = (p * (dp - delta)).astype(BF16)
        dq = dq + mm(ds, only(mask, k), NN)
        dk = dk + mm(ds, q_head, TN)
        dv = dv + mm(p.astype(BF16), d_head, TN)
    dq = (dq * HEAD**-0.5).astype(BF16)
    dk = dk.astype(BF16)
    dv = dv.astype(BF16)
    dn = mm(dq, weight(0), NT) + mm(dk, weight(1), NT) + mm(dv, weight(2), NT)
    for to in range(GROUP):
        part = slice(64 * to, 64 * to + 64)
        inv = inv_ref[part, 0:1]
        scaled = dn[part] * gain_ref[...]
        nhat = tok_ref[to, 1].astype(F32) * inv
        dx = inv * (scaled - nhat * jnp.mean(scaled * nhat, axis=-1, keepdims=True))
        out_ref[to, 1] = dx.astype(BF16)


VMEM = pl.BlockSpec(memory_space=pltpu.VMEM)
HBM = pl.BlockSpec(memory_space=pltpu.HBM)
SMEM = pl.BlockSpec(memory_space=pltpu.SMEM)


def call(body, shapes, inputs, name, in_specs=None, scratch=(), flops=10**6, mib=40, out=VMEM):
    return pl.pallas_call(
        body,
        out_shape=[jax.ShapeDtypeStruct(shape, kind) for shape, kind in shapes],
        in_specs=[VMEM] * len(inputs) if in_specs is None else in_specs,
        out_specs=[out] * len(shapes),
        scratch_shapes=list(scratch),
        compiler_params=pltpu.CompilerParams(vmem_limit_bytes=mib * 2**20),
        cost_estimate=pl.CostEstimate(flops=flops, bytes_accessed=10**6, transcendentals=0),
        name=name,
    )(*inputs)


def per_device(fwd_input, bwd_input, bwd_grad, norm_gain, w_query, w_key, w_value, w_out):
    seqs = lax.axis_size("seq")
    sections = lax.axis_size("section")
    deep = seqs // GROUP
    row_groups = [[GROUP * y + x for x in range(GROUP)] for y in range(deep)]
    columns = [[GROUP * y + x for y in range(deep)] for x in range(GROUP)]

    places = [(s, GROUP * (s % deep) + s // deep) for s in range(seqs)]
    own = lax.ppermute(w_out[0], "seq", places)
    qkv, = call(
        pack_weights,
        [((GROUP, 3, 32, 256), BF16)],
        (w_query[0], w_key[0], w_value[0]),
        "pack_weights",
        in_specs=[HBM] * 3,
        scratch=(pltpu.SemaphoreType.DMA((GROUP, 3)),),
        mib=63,
    )
    qkv = lax.all_to_all(qkv, "seq", 0, 0, axis_index_groups=row_groups, tiled=True)
    joined, = call(join_weights, [((GROUP, 4, 32, 256), BF16)], (qkv, own), "join_weights")
    weights = lax.all_gather(joined, "seq", axis_index_groups=columns)

    tokens, = call(
        pack_tokens,
        [((GROUP, 3, 64, 1024), BF16)],
        (joined, fwd_input[0], bwd_input[0], bwd_grad[0]),
        "pack_tokens",
        in_specs=[HBM] * 4,
        scratch=(
            pltpu.VMEM((64, 1024), F32),
            pltpu.SemaphoreType.DMA((GROUP, 2)),
            pltpu.SemaphoreType.DMA,
        ),
        mib=63,
    )
    tokens = lax.all_to_all(tokens, "seq", 0, 0, axis_index_groups=row_groups, tiled=True)
    normed, inv, bias = call(
        prepare,
        [((2, 256, 1024), BF16), ((256, 128), F32), ((HEADS, 256, 256), F32)],
        (tokens, norm_gain),
        "prepare",
    )
    parts, = call(
        layer,
        [((GROUP, 2, 64, 1024), BF16)],
        (tokens, normed, inv, bias, norm_gain, weights),
        "layer",
        in_specs=[VMEM] * 5 + [HBM],
        scratch=(
            pltpu.VMEM((4, deep, GROUP, 32, 256), BF16),
            pltpu.SemaphoreType.DMA((4,)),
        ),
        flops=15 * 10**8,
    )
    parts = lax.all_to_all(parts, "seq", 0, 0, axis_index_groups=row_groups, tiled=True)
    layer_out, input_grad = call(
        finish,
        [((64, 1024), BF16)] * 2,
        (parts, fwd_input[0], bwd_grad[0]),
        "finish",
    )
    ring = [(c, (c + 1) % sections) for c in range(sections)]
    next_input = lax.ppermute(layer_out, "section", ring)
    prev_grad = lax.ppermute(input_grad, "section", [(b, a) for a, b in ring])
    next_input, prev_grad = call(
        deliver,
        [((64, 1024), BF16), ((64, 1024), F32)],
        (next_input, prev_grad),
        "deliver",
    )
    return next_input[None], prev_grad[None]


def solution(mesh):
    placed = (
        P("section", "seq", None),
        P("section", "seq", None),
        P("section", "seq", None),
        P("section", None),
        P("section", "seq", None),
        P("section", "seq", None),
        P("section", "seq", None),
        P("section", "seq", None),
    )
    return jax.shard_map(
        per_device,
        mesh=mesh,
        in_specs=placed,
        out_specs=(P("section", "seq", None), P("section", "seq", None)),
        check_vma=False,
    )
```

```python
import functools
import math

import jax
import jax.numpy as jnp
from jax import lax
from jax.experimental import pallas as pl
from jax.experimental.pallas import tpu as pltpu
from jax.sharding import PartitionSpec as P

HEAD = 64
EPS = 1e-06
NEG = -1e30
GROUP = 4
HEADS = 4

F32 = jnp.float32
BF16 = jnp.bfloat16
NT = (((1,), (1,)), ((), ()))
NN = (((1,), (0,)), ((), ()))
TN = (((0,), (0,)), ((), ()))


def mm(a, b, dims):
    return lax.dot_general(a, b, dims, preferred_element_type=F32)


def pair_bias(rows):
    t = lax.broadcasted_iota(jnp.int32, (rows, rows), 0)
    u = lax.broadcasted_iota(jnp.int32, (rows, rows), 1)
    causal = u <= t
    apart = t ^ u
    one = causal & (apart < 64)
    two = causal & (apart < 128) & ((apart & 1) == 0)
    three = causal & (apart < 256) & ((apart & 3) == 0)
    all_three = jnp.where(one, math.log(3.0), math.log(2.0))
    one_more = jnp.where(one, math.log(2.0), 0.0)
    no_more = jnp.where(one, 0.0, NEG)
    biases = []
    for head in range(HEADS):
        second = two & ((t & 1) == head % 2)
        third = three & ((t & 3) == head)
        bias = jnp.where(third, one_more, no_more)
        biases.append(jnp.where(second, jnp.where(third, all_three, one_more), bias))
    return biases


def head_masks(rows):
    lane = lax.broadcasted_iota(jnp.int32, (rows, HEADS * HEAD), 1)
    return [(lane // HEAD) == head for head in range(HEADS)]


def only(mask, value):
    return jnp.where(mask, value, jnp.zeros((), value.dtype))


def pack_weights(q_hbm, k_hbm, v_hbm, out_ref, sems):
    copies = []
    for block in range(GROUP):
        columns = slice(256 * block, 256 * block + 256)
        for i, ref in enumerate((q_hbm, k_hbm, v_hbm)):
            source, target = ref.at[:, columns], out_ref.at[block, i]
            copies.append(pltpu.make_async_copy(source, target, sems.at[block, i]))
            copies[-1].start()
    for copy in copies:
        copy.wait()


def join_weights(qkv_ref, own_ref, out_ref):
    for block in range(GROUP):
        out_ref[block, :3] = qkv_ref[block]
        out_ref[block, 3] = own_ref[:, 256 * block : 256 * block + 256]


def pack_tokens(after_hbm, fwd_hbm, bwd_hbm, grad_hbm, out_ref, grad_ref, sems, grad_sem):
    del after_hbm
    first = pltpu.make_async_copy(grad_hbm, grad_ref, grad_sem)
    first.start()
    copies = []
    for to in range(GROUP):
        for i, ref in enumerate((fwd_hbm, bwd_hbm)):
            copies.append(pltpu.make_async_copy(ref, out_ref.at[to, i], sems.at[to, i]))
            copies[-1].start()
    first.wait()
    for to in range(GROUP):
        out_ref[to, 2] = grad_ref[...].astype(BF16)
    for copy in copies:
        copy.wait()


def finish(parts_ref, fwd_ref, grad_ref, next_ref, prev_ref):
    for which, own, out in ((0, fwd_ref, next_ref), (1, grad_ref, prev_ref)):
        total = own[...].astype(F32)
        for part in range(GROUP):
            total = total + parts_ref[part, which].astype(F32)
        out[...] = total.astype(BF16)


def prepare(tok_ref, gain_ref, normed_ref, inv_ref):
    for which in range(2):
        for part in range(GROUP):
            xf = tok_ref[part, which].astype(F32)
            inv = lax.rsqrt(jnp.mean(xf * xf, axis=-1, keepdims=True) + EPS)
            rows = slice(64 * part, 64 * part + 64)
            normed_ref[which, rows, :] = (xf * inv * gain_ref[...]).astype(BF16)
            if which == 1:
                inv_ref[rows, :] = jnp.broadcast_to(inv, (64, 128))


def deliver(next_ref, prev_ref, next_out, prev_out):
    next_out[...] = next_ref[...]
    prev_out[...] = prev_ref[...].astype(F32)


def layer(tok_ref, normed_ref, inv_ref, gain_ref, w_ref, out_ref, bias_ref):
    rows = GROUP * 64
    for head, bias in enumerate(pair_bias(rows)):
        bias_ref[head] = bias
    heads = head_masks(rows)
    scale = jnp.asarray(HEAD**-0.5, BF16)

    def weight(i):
        return w_ref[:, :, i].reshape(1024, 256)

    def out_weight(c):
        return w_ref[:, c, 3].reshape(256, 256)

    def projected(which):
        normed = normed_ref[which]
        q, k, v = [mm(normed, weight(i), NN).astype(BF16) for i in range(3)]
        return q * scale, k, v

    def prob_of(q_head, k, head):
        s = mm(q_head, k, NT) + bias_ref[head]
        top = jnp.max(s, axis=-1, keepdims=True)
        p = jnp.exp(s - top)
        return p * (1.0 / jnp.sum(p, axis=-1, keepdims=True))

    q, k, v = projected(0)
    attended = jnp.zeros((rows, 256), F32)
    for head in range(HEADS):
        p = prob_of(only(heads[head], q), k, head).astype(BF16)
        attended = attended + mm(p, only(heads[head], v), NN)
    attended = attended.astype(BF16)
    for c in range(4):
        part = mm(attended, out_weight(c), NN).astype(BF16)
        for to in range(GROUP):
            out_ref[to, 0, :, 256 * c : 256 * c + 256] = part[64 * to : 64 * to + 64]

    q, k, v = projected(1)
    grads = tok_ref[:, 2].reshape(rows, 1024)
    d_att = jnp.zeros((rows, 256), F32)
    for c in range(4):
        d_att = d_att + mm(grads[:, 256 * c : 256 * c + 256], out_weight(c), NT)
    d_att = d_att.astype(BF16)
    dq = jnp.zeros((rows, 256), F32)
    dk = jnp.zeros((rows, 256), F32)
    dv = jnp.zeros((rows, 256), F32)
    for head in range(HEADS):
        mask = heads[head]
        q_head = only(mask, q)
        p = prob_of(q_head, k, head)
        d_head = only(mask, d_att)
        dp = mm(d_head, v, NT)
        delta = jnp.sum(p * dp, axis=-1, keepdims=True)
        ds = (p * (dp - delta)).astype(BF16)
        dq = dq + mm(ds, only(mask, k), NN)
        dk = dk + mm(ds, q_head, TN)
        dv = dv + mm(p.astype(BF16), d_head, TN)
    dq = (dq * HEAD**-0.5).astype(BF16)
    dk = dk.astype(BF16)
    dv = dv.astype(BF16)
    dn = mm(dq, weight(0), NT) + mm(dk, weight(1), NT) + mm(dv, weight(2), NT)
    for to in range(GROUP):
        part = slice(64 * to, 64 * to + 64)
        inv = inv_ref[part, 0:1]
        scaled = dn[part] * gain_ref[...]
        nhat = tok_ref[to, 1].astype(F32) * inv
        dx = inv * (scaled - nhat * jnp.mean(scaled * nhat, axis=-1, keepdims=True))
        out_ref[to, 1] = dx.astype(BF16)


VMEM = pl.BlockSpec(memory_space=pltpu.VMEM)
HBM = pl.BlockSpec(memory_space=pltpu.HBM)
SMEM = pl.BlockSpec(memory_space=pltpu.SMEM)


def call(body, shapes, inputs, name, in_specs=None, scratch=(), flops=10**6, mib=40, out=VMEM):
    return pl.pallas_call(
        body,
        out_shape=[jax.ShapeDtypeStruct(shape, kind) for shape, kind in shapes],
        in_specs=[VMEM] * len(inputs) if in_specs is None else in_specs,
        out_specs=[out] * len(shapes),
        scratch_shapes=list(scratch),
        compiler_params=pltpu.CompilerParams(vmem_limit_bytes=mib * 2**20),
        cost_estimate=pl.CostEstimate(flops=flops, bytes_accessed=10**6, transcendentals=0),
        name=name,
    )(*inputs)


def per_device(fwd_input, bwd_input, bwd_grad, norm_gain, w_query, w_key, w_value, w_out):
    seqs = lax.axis_size("seq")
    sections = lax.axis_size("section")
    deep = seqs // GROUP
    row_groups = [[GROUP * y + x for x in range(GROUP)] for y in range(deep)]
    columns = [[GROUP * y + x for y in range(deep)] for x in range(GROUP)]

    places = [(s, GROUP * (s % deep) + s // deep) for s in range(seqs)]
    own = lax.ppermute(w_out[0], "seq", places)
    qkv, = call(
        pack_weights,
        [((GROUP, 3, 32, 256), BF16)],
        (w_query[0], w_key[0], w_value[0]),
        "pack_weights",
        in_specs=[HBM] * 3,
        scratch=(pltpu.SemaphoreType.DMA((GROUP, 3)),),
        mib=63,
    )
    qkv, own = lax.optimization_barrier((qkv, own))
    qkv = lax.all_to_all(qkv, "seq", 0, 0, axis_index_groups=row_groups, tiled=True)
    joined, = call(join_weights, [((GROUP, 4, 32, 256), BF16)], (qkv, own), "join_weights")
    weights = lax.all_gather(joined, "seq", axis_index_groups=columns)

    tokens, = call(
        pack_tokens,
        [((GROUP, 3, 64, 1024), BF16)],
        (joined, fwd_input[0], bwd_input[0], bwd_grad[0]),
        "pack_tokens",
        in_specs=[HBM] * 4,
        scratch=(
            pltpu.VMEM((64, 1024), F32),
            pltpu.SemaphoreType.DMA((GROUP, 2)),
            pltpu.SemaphoreType.DMA,
        ),
        mib=63,
    )
    tokens = lax.all_to_all(tokens, "seq", 0, 0, axis_index_groups=row_groups, tiled=True)
    normed, inv = call(
        prepare,
        [((2, 256, 1024), BF16), ((256, 128), F32)],
        (tokens, norm_gain),
        "prepare",
    )
    parts, = call(
        layer,
        [((GROUP, 2, 64, 1024), BF16)],
        (tokens, normed, inv, norm_gain, weights),
        "layer",
        scratch=(pltpu.VMEM((HEADS, 256, 256), F32),),
        flops=15 * 10**8,
    )
    parts = lax.all_to_all(parts, "seq", 0, 0, axis_index_groups=row_groups, tiled=True)
    layer_out, input_grad = call(
        finish,
        [((64, 1024), BF16)] * 2,
        (parts, fwd_input[0], bwd_grad[0]),
        "finish",
    )
    ring = [(c, (c + 1) % sections) for c in range(sections)]
    next_input = lax.ppermute(layer_out, "section", ring)
    prev_grad = lax.ppermute(input_grad, "section", [(b, a) for a, b in ring])
    next_input, prev_grad = call(
        deliver,
        [((64, 1024), BF16), ((64, 1024), F32)],
        (next_input, prev_grad),
        "deliver",
    )
    return next_input[None], prev_grad[None]


def solution(mesh):
    placed = (
        P("section", "seq", None),
        P("section", "seq", None),
        P("section", "seq", None),
        P("section", None),
        P("section", "seq", None),
        P("section", "seq", None),
        P("section", "seq", None),
        P("section", "seq", None),
    )
    return jax.shard_map(
        per_device,
        mesh=mesh,
        in_specs=placed,
        out_specs=(P("section", "seq", None), P("section", "seq", None)),
        check_vma=False,
    )
```

```python
import functools
import math

import jax
import jax.numpy as jnp
from jax import lax
from jax.experimental import pallas as pl
from jax.experimental.pallas import tpu as pltpu
from jax.sharding import PartitionSpec as P

HEAD = 64
EPS = 1e-06
NEG = -1e30
GROUP = 4
HEADS = 4

F32 = jnp.float32
BF16 = jnp.bfloat16
NT = (((1,), (1,)), ((), ()))
NN = (((1,), (0,)), ((), ()))
TN = (((0,), (0,)), ((), ()))


def mm(a, b, dims):
    return lax.dot_general(a, b, dims, preferred_element_type=F32)


def pair_bias(rows):
    t = lax.broadcasted_iota(jnp.int32, (rows, rows), 0)
    u = lax.broadcasted_iota(jnp.int32, (rows, rows), 1)
    causal = u <= t
    apart = t ^ u
    one = causal & (apart < 64)
    two = causal & (apart < 128) & ((apart & 1) == 0)
    three = causal & (apart < 256) & ((apart & 3) == 0)
    all_three = jnp.where(one, math.log(3.0), math.log(2.0))
    one_more = jnp.where(one, math.log(2.0), 0.0)
    no_more = jnp.where(one, 0.0, NEG)
    biases = []
    for head in range(HEADS):
        second = two & ((t & 1) == head % 2)
        third = three & ((t & 3) == head)
        bias = jnp.where(third, one_more, no_more)
        biases.append(jnp.where(second, jnp.where(third, all_three, one_more), bias))
    return biases


def head_masks(rows):
    lane = lax.broadcasted_iota(jnp.int32, (rows, HEADS * HEAD), 1)
    return [(lane // HEAD) == head for head in range(HEADS)]


def only(mask, value):
    return jnp.where(mask, value, jnp.zeros((), value.dtype))


def pack_weights(me_ref, q_hbm, k_hbm, v_hbm, out_ref, self_ref, sems):
    mine = pl.ds(pl.multiple_of(me_ref[0] * 256, 256), 256)
    copies = []
    for i, ref in enumerate((q_hbm, k_hbm, v_hbm)):
        copies.append(pltpu.make_async_copy(ref.at[:, mine], self_ref.at[i], sems.at[GROUP, i]))
        for block in range(GROUP):
            source, target = ref.at[:, 256 * block : 256 * block + 256], out_ref.at[block, i]
            copies.append(pltpu.make_async_copy(source, target, sems.at[block, i]))
    for copy in copies:
        copy.start()
    for copy in copies:
        copy.wait()


def join_weights(me_ref, qkv_ref, own_ref, out_ref):
    for k in range(1, GROUP):
        out_ref[3 * k - 3 : 3 * k] = qkv_ref[(me_ref[0] + k) % GROUP]
    for block in range(GROUP):
        out_ref[9 + block] = own_ref[:, 256 * block : 256 * block + 256]


def pack_tokens(after_hbm, fwd_hbm, bwd_hbm, grad_hbm, out_ref, grad_ref, sems, grad_sem):
    del after_hbm
    first = pltpu.make_async_copy(grad_hbm, grad_ref, grad_sem)
    first.start()
    copies = []
    for to in range(GROUP):
        for i, ref in enumerate((fwd_hbm, bwd_hbm)):
            copies.append(pltpu.make_async_copy(ref, out_ref.at[to, i], sems.at[to, i]))
            copies[-1].start()
    first.wait()
    for to in range(GROUP):
        out_ref[to, 2] = grad_ref[...].astype(BF16)
    for copy in copies:
        copy.wait()


def finish(parts_ref, fwd_ref, grad_ref, next_ref, prev_ref):
    for which, own, out in ((0, fwd_ref, next_ref), (1, grad_ref, prev_ref)):
        total = own[...].astype(F32)
        for part in range(GROUP):
            total = total + parts_ref[part, which].astype(F32)
        out[...] = total.astype(BF16)


def prepare(tok_ref, gain_ref, normed_ref, inv_ref):
    for which in range(2):
        for part in range(GROUP):
            xf = tok_ref[part, which].astype(F32)
            inv = lax.rsqrt(jnp.mean(xf * xf, axis=-1, keepdims=True) + EPS)
            rows = slice(64 * part, 64 * part + 64)
            normed_ref[which, rows, :] = (xf * inv * gain_ref[...]).astype(BF16)
            if which == 1:
                inv_ref[rows, :] = jnp.broadcast_to(inv, (64, 128))


def deliver(next_ref, prev_ref, next_out, prev_out):
    next_out[...] = next_ref[...]
    prev_out[...] = prev_ref[...].astype(F32)


def layer(me_ref, tok_ref, normed_ref, inv_ref, gain_ref, self_ref, rest_ref, *refs):
    out_ref, bias_ref, w_ref = refs
    rows = GROUP * 64
    for i in range(3):
        w_ref[i, :, me_ref[0]] = self_ref[:, i]
        for k in range(1, GROUP):
            w_ref[i, :, (me_ref[0] + k) % GROUP] = rest_ref[:, 3 * k - 3 + i]
    for head, bias in enumerate(pair_bias(rows)):
        bias_ref[head] = bias
    heads = head_masks(rows)
    scale = jnp.asarray(HEAD**-0.5, BF16)

    def weight(i):
        return w_ref[i].reshape(1024, 256)

    def out_weight(c):
        return rest_ref[:, 9 + c].reshape(256, 256)

    def projected(which):
        normed = normed_ref[which]
        q, k, v = [mm(normed, weight(i), NN).astype(BF16) for i in range(3)]
        return q * scale, k, v

    def prob_of(q_head, k, head):
        s = mm(q_head, k, NT) + bias_ref[head]
        top = jnp.max(s, axis=-1, keepdims=True)
        p = jnp.exp(s - top)
        return p * (1.0 / jnp.sum(p, axis=-1, keepdims=True))

    q, k, v = projected(0)
    attended = jnp.zeros((rows, 256), F32)
    for head in range(HEADS):
        p = prob_of(only(heads[head], q), k, head).astype(BF16)
        attended = attended + mm(p, only(heads[head], v), NN)
    attended = attended.astype(BF16)
    for c in range(4):
        part = mm(attended, out_weight(c), NN).astype(BF16)
        for to in range(GROUP):
            out_ref[to, 0, :, 256 * c : 256 * c + 256] = part[64 * to : 64 * to + 64]

    q, k, v = projected(1)
    grads = tok_ref[:, 2].reshape(rows, 1024)
    d_att = jnp.zeros((rows, 256), F32)
    for c in range(4):
        d_att = d_att + mm(grads[:, 256 * c : 256 * c + 256], out_weight(c), NT)
    d_att = d_att.astype(BF16)
    dq = jnp.zeros((rows, 256), F32)
    dk = jnp.zeros((rows, 256), F32)
    dv = jnp.zeros((rows, 256), F32)
    for head in range(HEADS):
        mask = heads[head]
        q_head = only(mask, q)
        p = prob_of(q_head, k, head)
        d_head = only(mask, d_att)
        dp = mm(d_head, v, NT)
        delta = jnp.sum(p * dp, axis=-1, keepdims=True)
        ds = (p * (dp - delta)).astype(BF16)
        dq = dq + mm(ds, only(mask, k), NN)
        dk = dk + mm(ds, q_head, TN)
        dv = dv + mm(p.astype(BF16), d_head, TN)
    dq = (dq * HEAD**-0.5).astype(BF16)
    dk = dk.astype(BF16)
    dv = dv.astype(BF16)
    dn = mm(dq, weight(0), NT) + mm(dk, weight(1), NT) + mm(dv, weight(2), NT)
    for to in range(GROUP):
        part = slice(64 * to, 64 * to + 64)
        inv = inv_ref[part, 0:1]
        scaled = dn[part] * gain_ref[...]
        nhat = tok_ref[to, 1].astype(F32) * inv
        dx = inv * (scaled - nhat * jnp.mean(scaled * nhat, axis=-1, keepdims=True))
        out_ref[to, 1] = dx.astype(BF16)


VMEM = pl.BlockSpec(memory_space=pltpu.VMEM)
HBM = pl.BlockSpec(memory_space=pltpu.HBM)
SMEM = pl.BlockSpec(memory_space=pltpu.SMEM)


def call(body, shapes, inputs, name, in_specs=None, scratch=(), flops=10**6, mib=40, out=VMEM):
    return pl.pallas_call(
        body,
        out_shape=[jax.ShapeDtypeStruct(shape, kind) for shape, kind in shapes],
        in_specs=[VMEM] * len(inputs) if in_specs is None else in_specs,
        out_specs=[out] * len(shapes),
        scratch_shapes=list(scratch),
        compiler_params=pltpu.CompilerParams(vmem_limit_bytes=mib * 2**20),
        cost_estimate=pl.CostEstimate(flops=flops, bytes_accessed=10**6, transcendentals=0),
        name=name,
    )(*inputs)


def per_device(fwd_input, bwd_input, bwd_grad, norm_gain, w_query, w_key, w_value, w_out):
    seqs = lax.axis_size("seq")
    sections = lax.axis_size("section")
    deep = seqs // GROUP
    row_groups = [[GROUP * y + x for x in range(GROUP)] for y in range(deep)]
    columns = [[GROUP * y + x for y in range(deep)] for x in range(GROUP)]

    me = (lax.axis_index("seq") % GROUP).reshape(1)

    qkv, self_part = call(
        pack_weights,
        [((GROUP, 3, 32, 256), BF16), ((3, 32, 256), BF16)],
        (me, w_query[0], w_key[0], w_value[0]),
        "pack_weights",
        in_specs=[SMEM] + [HBM] * 3,
        scratch=(pltpu.SemaphoreType.DMA((GROUP + 1, 3)),),
        mib=63,
    )
    self_part = lax.all_gather(self_part, "seq", axis_index_groups=columns)
    places = [(s, GROUP * (s % deep) + s // deep) for s in range(seqs)]
    own = lax.ppermute(w_out[0], "seq", places)
    qkv = lax.all_to_all(qkv, "seq", 0, 0, axis_index_groups=row_groups, tiled=True)
    joined, = call(
        join_weights,
        [((13, 32, 256), BF16)],
        (me, qkv, own),
        "join_weights",
        in_specs=[SMEM, VMEM, VMEM],
    )
    rest = lax.all_gather(joined, "seq", axis_index_groups=columns)

    tokens, = call(
        pack_tokens,
        [((GROUP, 3, 64, 1024), BF16)],
        (joined, fwd_input[0], bwd_input[0], bwd_grad[0]),
        "pack_tokens",
        in_specs=[HBM] * 4,
        scratch=(
            pltpu.VMEM((64, 1024), F32),
            pltpu.SemaphoreType.DMA((GROUP, 2)),
            pltpu.SemaphoreType.DMA,
        ),
        mib=63,
    )
    tokens = lax.all_to_all(tokens, "seq", 0, 0, axis_index_groups=row_groups, tiled=True)
    normed, inv = call(
        prepare,
        [((2, 256, 1024), BF16), ((256, 128), F32)],
        (tokens, norm_gain),
        "prepare",
    )
    parts, = call(
        layer,
        [((GROUP, 2, 64, 1024), BF16)],
        (me, tokens, normed, inv, norm_gain, self_part, rest),
        "layer",
        in_specs=[SMEM] + [VMEM] * 6,
        scratch=(
            pltpu.VMEM((HEADS, 256, 256), F32),
            pltpu.VMEM((3, deep, GROUP, 32, 256), BF16),
        ),
        flops=15 * 10**8,
    )
    parts = lax.all_to_all(parts, "seq", 0, 0, axis_index_groups=row_groups, tiled=True)
    layer_out, input_grad = call(
        finish,
        [((64, 1024), BF16)] * 2,
        (parts, fwd_input[0], bwd_grad[0]),
        "finish",
    )
    ring = [(c, (c + 1) % sections) for c in range(sections)]
    next_input = lax.ppermute(layer_out, "section", ring)
    prev_grad = lax.ppermute(input_grad, "section", [(b, a) for a, b in ring])
    next_input, prev_grad = call(
        deliver,
        [((64, 1024), BF16), ((64, 1024), F32)],
        (next_input, prev_grad),
        "deliver",
    )
    return next_input[None], prev_grad[None]


def solution(mesh):
    placed = (
        P("section", "seq", None),
        P("section", "seq", None),
        P("section", "seq", None),
        P("section", None),
        P("section", "seq", None),
        P("section", "seq", None),
        P("section", "seq", None),
        P("section", "seq", None),
    )
    return jax.shard_map(
        per_device,
        mesh=mesh,
        in_specs=placed,
        out_specs=(P("section", "seq", None), P("section", "seq", None)),
        check_vma=False,
    )
```

```python
import functools
import math

import jax
import jax.numpy as jnp
from jax import lax
from jax.experimental import pallas as pl
from jax.experimental.pallas import tpu as pltpu
from jax.sharding import PartitionSpec as P

HEAD = 64
EPS = 1e-06
NEG = -1e30
GROUP = 4
HEADS = 4

F32 = jnp.float32
BF16 = jnp.bfloat16
NT = (((1,), (1,)), ((), ()))
NN = (((1,), (0,)), ((), ()))
TN = (((0,), (0,)), ((), ()))


def mm(a, b, dims):
    return lax.dot_general(a, b, dims, preferred_element_type=F32)


def pair_bias(rows):
    t = lax.broadcasted_iota(jnp.int32, (rows, rows), 0)
    u = lax.broadcasted_iota(jnp.int32, (rows, rows), 1)
    causal = u <= t
    apart = t ^ u
    one = causal & (apart < 64)
    two = causal & (apart < 128) & ((apart & 1) == 0)
    three = causal & (apart < 256) & ((apart & 3) == 0)
    all_three = jnp.where(one, math.log(3.0), math.log(2.0))
    one_more = jnp.where(one, math.log(2.0), 0.0)
    no_more = jnp.where(one, 0.0, NEG)
    biases = []
    for head in range(HEADS):
        second = two & ((t & 1) == head % 2)
        third = three & ((t & 3) == head)
        bias = jnp.where(third, one_more, no_more)
        biases.append(jnp.where(second, jnp.where(third, all_three, one_more), bias))
    return biases


def head_masks(rows):
    lane = lax.broadcasted_iota(jnp.int32, (rows, HEADS * HEAD), 1)
    return [(lane // HEAD) == head for head in range(HEADS)]


def only(mask, value):
    return jnp.where(mask, value, jnp.zeros((), value.dtype))


def pack_weights(q_hbm, k_hbm, v_hbm, out_ref, sems):
    copies = []
    for block in range(GROUP):
        columns = slice(256 * block, 256 * block + 256)
        for i, ref in enumerate((q_hbm, k_hbm, v_hbm)):
            source, target = ref.at[:, columns], out_ref.at[block, i]
            copies.append(pltpu.make_async_copy(source, target, sems.at[block, i]))
            copies[-1].start()
    for copy in copies:
        copy.wait()


def pack_tokens(after_hbm, fwd_hbm, bwd_hbm, grad_hbm, out_ref, grad_ref, sems, grad_sem):
    del after_hbm
    first = pltpu.make_async_copy(grad_hbm, grad_ref, grad_sem)
    first.start()
    copies = []
    for to in range(GROUP):
        for i, ref in enumerate((fwd_hbm, bwd_hbm)):
            copies.append(pltpu.make_async_copy(ref, out_ref.at[to, i], sems.at[to, i]))
            copies[-1].start()
    first.wait()
    for to in range(GROUP):
        out_ref[to, 2] = grad_ref[...].astype(BF16)
    for copy in copies:
        copy.wait()


def finish(parts_ref, fwd_ref, grad_ref, next_ref, prev_ref):
    for which, own, out in ((0, fwd_ref, next_ref), (1, grad_ref, prev_ref)):
        total = own[...].astype(F32)
        for part in range(GROUP):
            total = total + parts_ref[part, which].astype(F32)
        out[...] = total.astype(BF16)


def prepare(tok_ref, gain_ref, normed_ref, inv_ref):
    for which in range(2):
        for part in range(GROUP):
            xf = tok_ref[part, which].astype(F32)
            inv = lax.rsqrt(jnp.mean(xf * xf, axis=-1, keepdims=True) + EPS)
            rows = slice(64 * part, 64 * part + 64)
            normed_ref[which, rows, :] = (xf * inv * gain_ref[...]).astype(BF16)
            if which == 1:
                inv_ref[rows, :] = jnp.broadcast_to(inv, (64, 128))


def deliver(next_ref, prev_ref, next_out, prev_out):
    next_out[...] = next_ref[...]
    prev_out[...] = prev_ref[...].astype(F32)


def layer(tok_ref, normed_ref, inv_ref, gain_ref, w_ref, own_ref, out_ref, bias_ref):
    rows = GROUP * 64
    for head, bias in enumerate(pair_bias(rows)):
        bias_ref[head] = bias
    heads = head_masks(rows)
    scale = jnp.asarray(HEAD**-0.5, BF16)

    def weight(i):
        return w_ref[:, :, i].reshape(1024, 256)

    def out_weight(c):
        return own_ref[:, :, 256 * c : 256 * c + 256].reshape(256, 256)

    def projected(which):
        normed = normed_ref[which]
        q, k, v = [mm(normed, weight(i), NN).astype(BF16) for i in range(3)]
        return q * scale, k, v

    def prob_of(q_head, k, head):
        s = mm(q_head, k, NT) + bias_ref[head]
        top = jnp.max(s, axis=-1, keepdims=True)
        p = jnp.exp(s - top)
        return p * (1.0 / jnp.sum(p, axis=-1, keepdims=True))

    q, k, v = projected(0)
    attended = jnp.zeros((rows, 256), F32)
    for head in range(HEADS):
        p = prob_of(only(heads[head], q), k, head).astype(BF16)
        attended = attended + mm(p, only(heads[head], v), NN)
    attended = attended.astype(BF16)
    for c in range(4):
        part = mm(attended, out_weight(c), NN).astype(BF16)
        for to in range(GROUP):
            out_ref[to, 0, :, 256 * c : 256 * c + 256] = part[64 * to : 64 * to + 64]

    q, k, v = projected(1)
    grads = tok_ref[:, 2].reshape(rows, 1024)
    d_att = jnp.zeros((rows, 256), F32)
    for c in range(4):
        d_att = d_att + mm(grads[:, 256 * c : 256 * c + 256], out_weight(c), NT)
    d_att = d_att.astype(BF16)
    dq = jnp.zeros((rows, 256), F32)
    dk = jnp.zeros((rows, 256), F32)
    dv = jnp.zeros((rows, 256), F32)
    for head in range(HEADS):
        mask = heads[head]
        q_head = only(mask, q)
        p = prob_of(q_head, k, head)
        d_head = only(mask, d_att)
        dp = mm(d_head, v, NT)
        delta = jnp.sum(p * dp, axis=-1, keepdims=True)
        ds = (p * (dp - delta)).astype(BF16)
        dq = dq + mm(ds, only(mask, k), NN)
        dk = dk + mm(ds, q_head, TN)
        dv = dv + mm(p.astype(BF16), d_head, TN)
    dq = (dq * HEAD**-0.5).astype(BF16)
    dk = dk.astype(BF16)
    dv = dv.astype(BF16)
    dn = mm(dq, weight(0), NT) + mm(dk, weight(1), NT) + mm(dv, weight(2), NT)
    for to in range(GROUP):
        part = slice(64 * to, 64 * to + 64)
        inv = inv_ref[part, 0:1]
        scaled = dn[part] * gain_ref[...]
        nhat = tok_ref[to, 1].astype(F32) * inv
        dx = inv * (scaled - nhat * jnp.mean(scaled * nhat, axis=-1, keepdims=True))
        out_ref[to, 1] = dx.astype(BF16)


VMEM = pl.BlockSpec(memory_space=pltpu.VMEM)
HBM = pl.BlockSpec(memory_space=pltpu.HBM)
SMEM = pl.BlockSpec(memory_space=pltpu.SMEM)


def call(body, shapes, inputs, name, in_specs=None, scratch=(), flops=10**6, mib=40, out=VMEM):
    return pl.pallas_call(
        body,
        out_shape=[jax.ShapeDtypeStruct(shape, kind) for shape, kind in shapes],
        in_specs=[VMEM] * len(inputs) if in_specs is None else in_specs,
        out_specs=[out] * len(shapes),
        scratch_shapes=list(scratch),
        compiler_params=pltpu.CompilerParams(vmem_limit_bytes=mib * 2**20),
        cost_estimate=pl.CostEstimate(flops=flops, bytes_accessed=10**6, transcendentals=0),
        name=name,
    )(*inputs)


def per_device(fwd_input, bwd_input, bwd_grad, norm_gain, w_query, w_key, w_value, w_out):
    seqs = lax.axis_size("seq")
    sections = lax.axis_size("section")
    deep = seqs // GROUP
    row_groups = [[GROUP * y + x for x in range(GROUP)] for y in range(deep)]
    columns = [[GROUP * y + x for y in range(deep)] for x in range(GROUP)]

    places = [(s, GROUP * (s % deep) + s // deep) for s in range(seqs)]
    own = lax.ppermute(w_out[0], "seq", places)
    qkv, = call(
        pack_weights,
        [((GROUP, 3, 32, 256), BF16)],
        (w_query[0], w_key[0], w_value[0]),
        "pack_weights",
        in_specs=[HBM] * 3,
        scratch=(pltpu.SemaphoreType.DMA((GROUP, 3)),),
        mib=63,
    )
    qkv = lax.all_to_all(qkv, "seq", 0, 0, axis_index_groups=row_groups, tiled=True)
    weights = lax.all_gather(qkv, "seq", axis_index_groups=columns)

    tokens, = call(
        pack_tokens,
        [((GROUP, 3, 64, 1024), BF16)],
        (qkv, fwd_input[0], bwd_input[0], bwd_grad[0]),
        "pack_tokens",
        in_specs=[HBM] * 4,
        scratch=(
            pltpu.VMEM((64, 1024), F32),
            pltpu.SemaphoreType.DMA((GROUP, 2)),
            pltpu.SemaphoreType.DMA,
        ),
        mib=63,
    )
    own, tokens = lax.optimization_barrier((own, tokens))
    own = lax.all_gather(own, "seq", axis_index_groups=columns)
    tokens = lax.all_to_all(tokens, "seq", 0, 0, axis_index_groups=row_groups, tiled=True)
    normed, inv = call(
        prepare,
        [((2, 256, 1024), BF16), ((256, 128), F32)],
        (tokens, norm_gain),
        "prepare",
    )
    parts, = call(
        layer,
        [((GROUP, 2, 64, 1024), BF16)],
        (tokens, normed, inv, norm_gain, weights, own),
        "layer",
        scratch=(pltpu.VMEM((HEADS, 256, 256), F32),),
        flops=15 * 10**8,
    )
    parts = lax.all_to_all(parts, "seq", 0, 0, axis_index_groups=row_groups, tiled=True)
    layer_out, input_grad = call(
        finish,
        [((64, 1024), BF16)] * 2,
        (parts, fwd_input[0], bwd_grad[0]),
        "finish",
    )
    ring = [(c, (c + 1) % sections) for c in range(sections)]
    next_input = lax.ppermute(layer_out, "section", ring)
    prev_grad = lax.ppermute(input_grad, "section", [(b, a) for a, b in ring])
    next_input, prev_grad = call(
        deliver,
        [((64, 1024), BF16), ((64, 1024), F32)],
        (next_input, prev_grad),
        "deliver",
    )
    return next_input[None], prev_grad[None]


def solution(mesh):
    placed = (
        P("section", "seq", None),
        P("section", "seq", None),
        P("section", "seq", None),
        P("section", None),
        P("section", "seq", None),
        P("section", "seq", None),
        P("section", "seq", None),
        P("section", "seq", None),
    )
    return jax.shard_map(
        per_device,
        mesh=mesh,
        in_specs=placed,
        out_specs=(P("section", "seq", None), P("section", "seq", None)),
        check_vma=False,
    )
```

```python
import functools
import math

import jax
import jax.numpy as jnp
from jax import lax
from jax.experimental import pallas as pl
from jax.experimental.pallas import tpu as pltpu
from jax.sharding import PartitionSpec as P

HEAD = 64
EPS = 1e-06
NEG = -1e30
GROUP = 4
HEADS = 4

F32 = jnp.float32
BF16 = jnp.bfloat16
NT = (((1,), (1,)), ((), ()))
NN = (((1,), (0,)), ((), ()))
TN = (((0,), (0,)), ((), ()))


def mm(a, b, dims):
    return lax.dot_general(a, b, dims, preferred_element_type=F32)


def pair_bias(rows):
    t = lax.broadcasted_iota(jnp.int32, (rows, rows), 0)
    u = lax.broadcasted_iota(jnp.int32, (rows, rows), 1)
    causal = u <= t
    apart = t ^ u
    one = causal & (apart < 64)
    two = causal & (apart < 128) & ((apart & 1) == 0)
    three = causal & (apart < 256) & ((apart & 3) == 0)
    all_three = jnp.where(one, math.log(3.0), math.log(2.0))
    one_more = jnp.where(one, math.log(2.0), 0.0)
    no_more = jnp.where(one, 0.0, NEG)
    biases = []
    for head in range(HEADS):
        second = two & ((t & 1) == head % 2)
        third = three & ((t & 3) == head)
        bias = jnp.where(third, one_more, no_more)
        biases.append(jnp.where(second, jnp.where(third, all_three, one_more), bias))
    return biases


def head_masks(rows):
    lane = lax.broadcasted_iota(jnp.int32, (rows, HEADS * HEAD), 1)
    return [(lane // HEAD) == head for head in range(HEADS)]


def only(mask, value):
    return jnp.where(mask, value, jnp.zeros((), value.dtype))


def pack_weights(q_hbm, k_hbm, v_hbm, out_ref, sems):
    copies = []
    for block in range(GROUP):
        columns = slice(256 * block, 256 * block + 256)
        for i, ref in enumerate((q_hbm, k_hbm, v_hbm)):
            source, target = ref.at[:, columns], out_ref.at[block, i]
            copies.append(pltpu.make_async_copy(source, target, sems.at[block, i]))
            copies[-1].start()
    for copy in copies:
        copy.wait()


def pack_tokens(after_hbm, fwd_hbm, bwd_hbm, grad_hbm, out_ref, grad_ref, sems, grad_sem):
    del after_hbm
    first = pltpu.make_async_copy(grad_hbm, grad_ref, grad_sem)
    first.start()
    copies = []
    for to in range(GROUP):
        for i, ref in enumerate((fwd_hbm, bwd_hbm)):
            copies.append(pltpu.make_async_copy(ref, out_ref.at[to, i], sems.at[to, i]))
            copies[-1].start()
    first.wait()
    for to in range(GROUP):
        out_ref[to, 2] = grad_ref[...].astype(BF16)
    for copy in copies:
        copy.wait()


def finish(parts_ref, fwd_ref, grad_ref, next_ref, prev_ref):
    for which, own, out in ((0, fwd_ref, next_ref), (1, grad_ref, prev_ref)):
        total = own[...].astype(F32)
        for part in range(GROUP):
            total = total + parts_ref[part, which].astype(F32)
        out[...] = total.astype(BF16)


def prepare(tok_ref, gain_ref, normed_ref, inv_ref):
    for which in range(2):
        for part in range(GROUP):
            xf = tok_ref[part, which].astype(F32)
            inv = lax.rsqrt(jnp.mean(xf * xf, axis=-1, keepdims=True) + EPS)
            rows = slice(64 * part, 64 * part + 64)
            normed_ref[which, rows, :] = (xf * inv * gain_ref[...]).astype(BF16)
            if which == 1:
                inv_ref[rows, :] = jnp.broadcast_to(inv, (64, 128))


def deliver(next_ref, prev_ref, next_out, prev_out):
    next_out[...] = next_ref[...]
    prev_out[...] = prev_ref[...].astype(F32)


def layer(tok_ref, normed_ref, inv_ref, gain_ref, w_ref, own_ref, out_ref, bias_ref):
    rows = GROUP * 64
    for head, bias in enumerate(pair_bias(rows)):
        bias_ref[head] = bias
    heads = head_masks(rows)
    scale = jnp.asarray(HEAD**-0.5, BF16)

    def weight(i):
        return w_ref[:, :, i].reshape(1024, 256)

    def out_weight(c):
        return own_ref[:, :, 256 * c : 256 * c + 256].reshape(256, 256)

    def projected(which):
        normed = normed_ref[which]
        q, k, v = [mm(normed, weight(i), NN).astype(BF16) for i in range(3)]
        return q * scale, k, v

    def prob_of(q_head, k, head):
        s = mm(q_head, k, NT) + bias_ref[head]
        top = jnp.max(s, axis=-1, keepdims=True)
        p = jnp.exp(s - top)
        return p * (1.0 / jnp.sum(p, axis=-1, keepdims=True))

    q, k, v = projected(0)
    attended = jnp.zeros((rows, 256), F32)
    for head in range(HEADS):
        p = prob_of(only(heads[head], q), k, head).astype(BF16)
        attended = attended + mm(p, only(heads[head], v), NN)
    attended = attended.astype(BF16)
    for c in range(4):
        part = mm(attended, out_weight(c), NN).astype(BF16)
        for to in range(GROUP):
            out_ref[to, 0, :, 256 * c : 256 * c + 256] = part[64 * to : 64 * to + 64]

    q, k, v = projected(1)
    grads = tok_ref[:, 2].reshape(rows, 1024)
    d_att = jnp.zeros((rows, 256), F32)
    for c in range(4):
        d_att = d_att + mm(grads[:, 256 * c : 256 * c + 256], out_weight(c), NT)
    d_att = d_att.astype(BF16)
    dq = jnp.zeros((rows, 256), F32)
    dk = jnp.zeros((rows, 256), F32)
    dv = jnp.zeros((rows, 256), F32)
    for head in range(HEADS):
        mask = heads[head]
        q_head = only(mask, q)
        p = prob_of(q_head, k, head)
        d_head = only(mask, d_att)
        dp = mm(d_head, v, NT)
        delta = jnp.sum(p * dp, axis=-1, keepdims=True)
        ds = (p * (dp - delta)).astype(BF16)
        dq = dq + mm(ds, only(mask, k), NN)
        dk = dk + mm(ds, q_head, TN)
        dv = dv + mm(p.astype(BF16), d_head, TN)
    dq = (dq * HEAD**-0.5).astype(BF16)
    dk = dk.astype(BF16)
    dv = dv.astype(BF16)
    dn = mm(dq, weight(0), NT) + mm(dk, weight(1), NT) + mm(dv, weight(2), NT)
    for to in range(GROUP):
        part = slice(64 * to, 64 * to + 64)
        inv = inv_ref[part, 0:1]
        scaled = dn[part] * gain_ref[...]
        nhat = tok_ref[to, 1].astype(F32) * inv
        dx = inv * (scaled - nhat * jnp.mean(scaled * nhat, axis=-1, keepdims=True))
        out_ref[to, 1] = dx.astype(BF16)


VMEM = pl.BlockSpec(memory_space=pltpu.VMEM)
HBM = pl.BlockSpec(memory_space=pltpu.HBM)
SMEM = pl.BlockSpec(memory_space=pltpu.SMEM)


def call(body, shapes, inputs, name, in_specs=None, scratch=(), flops=10**6, mib=40, out=VMEM):
    return pl.pallas_call(
        body,
        out_shape=[jax.ShapeDtypeStruct(shape, kind) for shape, kind in shapes],
        in_specs=[VMEM] * len(inputs) if in_specs is None else in_specs,
        out_specs=[out] * len(shapes),
        scratch_shapes=list(scratch),
        compiler_params=pltpu.CompilerParams(vmem_limit_bytes=mib * 2**20),
        cost_estimate=pl.CostEstimate(flops=flops, bytes_accessed=10**6, transcendentals=0),
        name=name,
    )(*inputs)


def per_device(fwd_input, bwd_input, bwd_grad, norm_gain, w_query, w_key, w_value, w_out):
    seqs = lax.axis_size("seq")
    sections = lax.axis_size("section")
    deep = seqs // GROUP
    row_groups = [[GROUP * y + x for x in range(GROUP)] for y in range(deep)]
    columns = [[GROUP * y + x for y in range(deep)] for x in range(GROUP)]

    places = [(s, GROUP * (s % deep) + s // deep) for s in range(seqs)]
    own = lax.ppermute(w_out[0], "seq", places)
    qkv, = call(
        pack_weights,
        [((GROUP, 3, 32, 256), BF16)],
        (w_query[0], w_key[0], w_value[0]),
        "pack_weights",
        in_specs=[HBM] * 3,
        scratch=(pltpu.SemaphoreType.DMA((GROUP, 3)),),
        mib=63,
    )
    qkv = lax.all_to_all(qkv, "seq", 0, 0, axis_index_groups=row_groups, tiled=True)
    weights = lax.all_gather(qkv, "seq", axis_index_groups=columns)

    tokens, = call(
        pack_tokens,
        [((GROUP, 3, 64, 1024), BF16)],
        (qkv, fwd_input[0], bwd_input[0], bwd_grad[0]),
        "pack_tokens",
        in_specs=[HBM] * 4,
        scratch=(
            pltpu.VMEM((64, 1024), F32),
            pltpu.SemaphoreType.DMA((GROUP, 2)),
            pltpu.SemaphoreType.DMA,
        ),
        mib=63,
    )
    own, _ = lax.optimization_barrier((own, tokens))
    own = lax.all_gather(own, "seq", axis_index_groups=columns)
    tokens = lax.all_to_all(tokens, "seq", 0, 0, axis_index_groups=row_groups, tiled=True)
    normed, inv = call(
        prepare,
        [((2, 256, 1024), BF16), ((256, 128), F32)],
        (tokens, norm_gain),
        "prepare",
    )
    parts, = call(
        layer,
        [((GROUP, 2, 64, 1024), BF16)],
        (tokens, normed, inv, norm_gain, weights, own),
        "layer",
        scratch=(pltpu.VMEM((HEADS, 256, 256), F32),),
        flops=15 * 10**8,
    )
    parts = lax.all_to_all(parts, "seq", 0, 0, axis_index_groups=row_groups, tiled=True)
    layer_out, input_grad = call(
        finish,
        [((64, 1024), BF16)] * 2,
        (parts, fwd_input[0], bwd_grad[0]),
        "finish",
    )
    ring = [(c, (c + 1) % sections) for c in range(sections)]
    next_input = lax.ppermute(layer_out, "section", ring)
    prev_grad = lax.ppermute(input_grad, "section", [(b, a) for a, b in ring])
    next_input, prev_grad = call(
        deliver,
        [((64, 1024), BF16), ((64, 1024), F32)],
        (next_input, prev_grad),
        "deliver",
    )
    return next_input[None], prev_grad[None]


def solution(mesh):
    placed = (
        P("section", "seq", None),
        P("section", "seq", None),
        P("section", "seq", None),
        P("section", None),
        P("section", "seq", None),
        P("section", "seq", None),
        P("section", "seq", None),
        P("section", "seq", None),
    )
    return jax.shard_map(
        per_device,
        mesh=mesh,
        in_specs=placed,
        out_specs=(P("section", "seq", None), P("section", "seq", None)),
        check_vma=False,
    )
```

```python
import functools
import math

import jax
import jax.numpy as jnp
from jax import lax
from jax.experimental import pallas as pl
from jax.experimental.pallas import tpu as pltpu
from jax.sharding import PartitionSpec as P

HEAD = 64
EPS = 1e-06
NEG = -1e30
GROUP = 4
HEADS = 4

F32 = jnp.float32
BF16 = jnp.bfloat16
NT = (((1,), (1,)), ((), ()))
NN = (((1,), (0,)), ((), ()))
TN = (((0,), (0,)), ((), ()))


def mm(a, b, dims):
    return lax.dot_general(a, b, dims, preferred_element_type=F32)


def pair_bias(rows):
    t = lax.broadcasted_iota(jnp.int32, (rows, rows), 0)
    u = lax.broadcasted_iota(jnp.int32, (rows, rows), 1)
    causal = u <= t
    apart = t ^ u
    one = causal & (apart < 64)
    two = causal & (apart < 128) & ((apart & 1) == 0)
    three = causal & (apart < 256) & ((apart & 3) == 0)
    all_three = jnp.where(one, math.log(3.0), math.log(2.0))
    one_more = jnp.where(one, math.log(2.0), 0.0)
    no_more = jnp.where(one, 0.0, NEG)
    biases = []
    for head in range(HEADS):
        second = two & ((t & 1) == head % 2)
        third = three & ((t & 3) == head)
        bias = jnp.where(third, one_more, no_more)
        biases.append(jnp.where(second, jnp.where(third, all_three, one_more), bias))
    return biases


def head_masks(rows):
    lane = lax.broadcasted_iota(jnp.int32, (rows, HEADS * HEAD), 1)
    return [(lane // HEAD) == head for head in range(HEADS)]


def only(mask, value):
    return jnp.where(mask, value, jnp.zeros((), value.dtype))


def pack_weights(q_hbm, k_hbm, v_hbm, out_ref, sems):
    copies = []
    for block in range(GROUP):
        columns = slice(256 * block, 256 * block + 256)
        for i, ref in enumerate((q_hbm, k_hbm, v_hbm)):
            source, target = ref.at[:, columns], out_ref.at[block, i]
            copies.append(pltpu.make_async_copy(source, target, sems.at[block, i]))
            copies[-1].start()
    for copy in copies:
        copy.wait()


def pack_tokens(after_hbm, fwd_hbm, bwd_hbm, grad_hbm, out_hbm, grad_ref, low_ref, sems, in_sems):
    del after_hbm
    loads = [
        pltpu.make_async_copy(fwd_hbm, low_ref.at[0], in_sems.at[0]),
        pltpu.make_async_copy(bwd_hbm, low_ref.at[1], in_sems.at[1]),
        pltpu.make_async_copy(grad_hbm, grad_ref, in_sems.at[2]),
    ]
    for load in loads:
        load.start()
    copies = []
    for i, load in enumerate(loads):
        load.wait()
        if i == 2:
            low_ref[2] = grad_ref[...].astype(BF16)
        for to in range(GROUP):
            copies.append(pltpu.make_async_copy(low_ref.at[i], out_hbm.at[to, i], sems.at[to, i]))
            copies[-1].start()
    for copy in copies:
        copy.wait()


def finish(parts_ref, fwd_ref, grad_ref, next_ref, prev_ref):
    for which, own, out in ((0, fwd_ref, next_ref), (1, grad_ref, prev_ref)):
        total = own[...].astype(F32)
        for part in range(GROUP):
            total = total + parts_ref[part, which].astype(F32)
        out[...] = total.astype(BF16)


def prepare(tok_ref, gain_ref, normed_ref, inv_ref):
    for which in range(2):
        for part in range(GROUP):
            xf = tok_ref[part, which].astype(F32)
            inv = lax.rsqrt(jnp.mean(xf * xf, axis=-1, keepdims=True) + EPS)
            rows = slice(64 * part, 64 * part + 64)
            normed_ref[which, rows, :] = (xf * inv * gain_ref[...]).astype(BF16)
            if which == 1:
                inv_ref[rows, :] = jnp.broadcast_to(inv, (64, 128))


def deliver(next_ref, prev_ref, next_out, prev_out):
    next_out[...] = next_ref[...]
    prev_out[...] = prev_ref[...].astype(F32)


def layer(tok_ref, normed_ref, inv_ref, gain_ref, w_ref, own_ref, out_ref, bias_ref):
    rows = GROUP * 64
    for head, bias in enumerate(pair_bias(rows)):
        bias_ref[head] = bias
    heads = head_masks(rows)
    scale = jnp.asarray(HEAD**-0.5, BF16)

    def weight(i):
        return w_ref[:, :, i].reshape(1024, 256)

    def out_weight(c):
        return own_ref[:, :, 256 * c : 256 * c + 256].reshape(256, 256)

    def projected(which):
        normed = normed_ref[which]
        q, k, v = [mm(normed, weight(i), NN).astype(BF16) for i in range(3)]
        return q * scale, k, v

    def prob_of(q_head, k, head):
        s = mm(q_head, k, NT) + bias_ref[head]
        top = jnp.max(s, axis=-1, keepdims=True)
        p = jnp.exp(s - top)
        return p * (1.0 / jnp.sum(p, axis=-1, keepdims=True))

    q, k, v = projected(0)
    attended = jnp.zeros((rows, 256), F32)
    for head in range(HEADS):
        p = prob_of(only(heads[head], q), k, head).astype(BF16)
        attended = attended + mm(p, only(heads[head], v), NN)
    attended = attended.astype(BF16)
    for c in range(4):
        part = mm(attended, out_weight(c), NN).astype(BF16)
        for to in range(GROUP):
            out_ref[to, 0, :, 256 * c : 256 * c + 256] = part[64 * to : 64 * to + 64]

    q, k, v = projected(1)
    grads = tok_ref[:, 2].reshape(rows, 1024)
    d_att = jnp.zeros((rows, 256), F32)
    for c in range(4):
        d_att = d_att + mm(grads[:, 256 * c : 256 * c + 256], out_weight(c), NT)
    d_att = d_att.astype(BF16)
    dq = jnp.zeros((rows, 256), F32)
    dk = jnp.zeros((rows, 256), F32)
    dv = jnp.zeros((rows, 256), F32)
    for head in range(HEADS):
        mask = heads[head]
        q_head = only(mask, q)
        p = prob_of(q_head, k, head)
        d_head = only(mask, d_att)
        dp = mm(d_head, v, NT)
        delta = jnp.sum(p * dp, axis=-1, keepdims=True)
        ds = (p * (dp - delta)).astype(BF16)
        dq = dq + mm(ds, only(mask, k), NN)
        dk = dk + mm(ds, q_head, TN)
        dv = dv + mm(p.astype(BF16), d_head, TN)
    dq = (dq * HEAD**-0.5).astype(BF16)
    dk = dk.astype(BF16)
    dv = dv.astype(BF16)
    dn = mm(dq, weight(0), NT) + mm(dk, weight(1), NT) + mm(dv, weight(2), NT)
    for to in range(GROUP):
        part = slice(64 * to, 64 * to + 64)
        inv = inv_ref[part, 0:1]
        scaled = dn[part] * gain_ref[...]
        nhat = tok_ref[to, 1].astype(F32) * inv
        dx = inv * (scaled - nhat * jnp.mean(scaled * nhat, axis=-1, keepdims=True))
        out_ref[to, 1] = dx.astype(BF16)


VMEM = pl.BlockSpec(memory_space=pltpu.VMEM)
HBM = pl.BlockSpec(memory_space=pltpu.HBM)
SMEM = pl.BlockSpec(memory_space=pltpu.SMEM)


def call(body, shapes, inputs, name, in_specs=None, scratch=(), flops=10**6, mib=40, out=VMEM):
    return pl.pallas_call(
        body,
        out_shape=[jax.ShapeDtypeStruct(shape, kind) for shape, kind in shapes],
        in_specs=[VMEM] * len(inputs) if in_specs is None else in_specs,
        out_specs=[out] * len(shapes),
        scratch_shapes=list(scratch),
        compiler_params=pltpu.CompilerParams(vmem_limit_bytes=mib * 2**20),
        cost_estimate=pl.CostEstimate(flops=flops, bytes_accessed=10**6, transcendentals=0),
        name=name,
    )(*inputs)


def per_device(fwd_input, bwd_input, bwd_grad, norm_gain, w_query, w_key, w_value, w_out):
    seqs = lax.axis_size("seq")
    sections = lax.axis_size("section")
    deep = seqs // GROUP
    row_groups = [[GROUP * y + x for x in range(GROUP)] for y in range(deep)]
    columns = [[GROUP * y + x for y in range(deep)] for x in range(GROUP)]

    places = [(s, GROUP * (s % deep) + s // deep) for s in range(seqs)]
    own = lax.ppermute(w_out[0], "seq", places)
    qkv, = call(
        pack_weights,
        [((GROUP, 3, 32, 256), BF16)],
        (w_query[0], w_key[0], w_value[0]),
        "pack_weights",
        in_specs=[HBM] * 3,
        scratch=(pltpu.SemaphoreType.DMA((GROUP, 3)),),
        mib=63,
    )
    qkv = lax.all_to_all(qkv, "seq", 0, 0, axis_index_groups=row_groups, tiled=True)
    weights = lax.all_gather(qkv, "seq", axis_index_groups=columns)

    tokens, = call(
        pack_tokens,
        [((GROUP, 3, 64, 1024), BF16)],
        (qkv, fwd_input[0], bwd_input[0], bwd_grad[0]),
        "pack_tokens",
        in_specs=[HBM] * 4,
        scratch=(
            pltpu.VMEM((64, 1024), F32),
            pltpu.VMEM((3, 64, 1024), BF16),
            pltpu.SemaphoreType.DMA((GROUP, 3)),
            pltpu.SemaphoreType.DMA((3,)),
        ),
        mib=63,
        out=HBM,
    )
    own, tokens = lax.optimization_barrier((own, tokens))
    own = lax.all_gather(own, "seq", axis_index_groups=columns)
    tokens = lax.all_to_all(tokens, "seq", 0, 0, axis_index_groups=row_groups, tiled=True)
    normed, inv = call(
        prepare,
        [((2, 256, 1024), BF16), ((256, 128), F32)],
        (tokens, norm_gain),
        "prepare",
    )
    parts, = call(
        layer,
        [((GROUP, 2, 64, 1024), BF16)],
        (tokens, normed, inv, norm_gain, weights, own),
        "layer",
        scratch=(pltpu.VMEM((HEADS, 256, 256), F32),),
        flops=15 * 10**8,
    )
    parts = lax.all_to_all(parts, "seq", 0, 0, axis_index_groups=row_groups, tiled=True)
    layer_out, input_grad = call(
        finish,
        [((64, 1024), BF16)] * 2,
        (parts, fwd_input[0], bwd_grad[0]),
        "finish",
    )
    ring = [(c, (c + 1) % sections) for c in range(sections)]
    next_input = lax.ppermute(layer_out, "section", ring)
    prev_grad = lax.ppermute(input_grad, "section", [(b, a) for a, b in ring])
    next_input, prev_grad = call(
        deliver,
        [((64, 1024), BF16), ((64, 1024), F32)],
        (next_input, prev_grad),
        "deliver",
    )
    return next_input[None], prev_grad[None]


def solution(mesh):
    placed = (
        P("section", "seq", None),
        P("section", "seq", None),
        P("section", "seq", None),
        P("section", None),
        P("section", "seq", None),
        P("section", "seq", None),
        P("section", "seq", None),
        P("section", "seq", None),
    )
    return jax.shard_map(
        per_device,
        mesh=mesh,
        in_specs=placed,
        out_specs=(P("section", "seq", None), P("section", "seq", None)),
        check_vma=False,
    )
```
